128 devices in a mesh: section: 4 (over z_lo, core), fsdp: 32 (over y, x, z_hi).
Axes of the slice: x: 4, y: 4, z: 4 (z_hi: 2, z_lo: 2; z = z_hi * 2 + z_lo), core: 2. Of those that a mesh axis runs over, the one named last changes fastest.
Arguments:
- fwd_in: bfloat16 [4, 512, 6144], P('section', 'fsdp'), may hold values from -6 to 6
- saved: bfloat16 [4, 512, 6144], P('section', 'fsdp'), may hold values from -6 to 6
- gain: float32 [4, 6144], P('section'), may hold values from 0.1 to 1.9
- w_in: bfloat16 [4, 6144, 12288], P('section', None, 'fsdp'), may hold values from -0.078125 to 0.078125
- w_out: bfloat16 [4, 12288, 6144], P('section', 'fsdp'), may hold values from -0.0546875 to 0.0546875
- cot_in: bfloat16 [4, 512, 6144], P('section', 'fsdp'), may hold values from -6 to 6
Outputs:
- fwd_arrive: bfloat16 [4, 512, 6144], P('section', 'fsdp')
- cot_arrive: bfloat16 [4, 512, 6144], P('section', 'fsdp')
- grad_in: bfloat16 [4, 6144, 12288], P('section', None, 'fsdp')
- grad_out: bfloat16 [4, 12288, 6144], P('section', 'fsdp')
The draws below stay inside these ranges and needn't reach their ends.
All inputs are finite; a program needn't handle non-finite values.
Results may differ from the reference program's by a relative error of at most 0.015.
Values may be sent and summed in bfloat16 or wider, within the bound.
A program may use at most 192 MiB of HBM per device.

```python
import math
import jax
import jax.numpy as jnp
from jax import lax

D = 6144
FF = 12288
M = 512
N_SECTION = 4
N_FSDP = 32


def steps_of(own_key, shape, pieces, least, high):
    level = 1.0
    for dim, shards_of in pieces:
        heights = jax.random.uniform(jax.random.fold_in(jax.random.fold_in(own_key, 6), dim), (shards_of,), jnp.float32, least / len(pieces), high / len(pieces))
        level = level * jnp.repeat(jnp.exp(heights), shape[dim] // shards_of).reshape((-1,) + (1,) * (len(shape) - 1 - dim))
    return level


def centred(stream_key, extent, spread, bound, split=(), kind=jnp.bfloat16):
    values = spread * jax.random.normal(stream_key, extent, jnp.float32)
    if split:
        values = values * steps_of(stream_key, extent, split, -0.22, 0.18)
    return jnp.clip(values, -bound, bound).astype(kind)


def setup_inputs(seed: int = 0) -> dict:
    streams_of = jax.random.split(jax.random.key(seed), 7)
    fwd_in = centred(streams_of[0], (N_SECTION, M, D), 1.0, 6.0, ((0, 4), (1, 32)))
    saved = centred(streams_of[1], (N_SECTION, M, D), 1.0, 6.0, ((0, 4), (1, 32)))
    gain = jnp.clip(1.0 + 0.18 * jax.random.normal(streams_of[2], (N_SECTION, D), jnp.float32), 0.1, 1.9)
    w_in = centred(streams_of[3], (N_SECTION, D, FF), D ** -0.5, 0.078125, ((0, 4), (2, 32)))
    w_out = centred(streams_of[4], (N_SECTION, FF, D), FF ** -0.5, 0.0546875, ((0, 4), (1, 32)))
    cot_in = centred(streams_of[5], (N_SECTION, M, D), 1.0, 6.0, ((0, 4), (1, 32)))
    return dict(fwd_in=fwd_in, saved=saved, gain=gain, w_in=w_in, w_out=w_out, cot_in=cot_in)


epsilon = 1e-06

def normalize(rows):
    values = rows.astype(jnp.float32)
    center = values - lax.optimization_barrier(jnp.mean(values, axis=-1, keepdims=True))
    scale = lax.rsqrt(lax.optimization_barrier(jnp.mean(center * center, axis=-1, keepdims=True)) + epsilon)
    return (center * scale, scale)

def gelu_slope(pre):
    cdf = 0.5 * (1.0 + jax.scipy.special.erf(pre * (1.0 / math.sqrt(2.0))))
    return cdf + pre * jnp.exp(-0.5 * pre * pre) * (1.0 / math.sqrt(2.0 * math.pi))

def norm_back(unit, scale, gain_row, incoming):
    grad_unit = incoming * gain_row
    mean_one = lax.optimization_barrier(jnp.mean(grad_unit, axis=-1, keepdims=True))
    mean_two = lax.optimization_barrier(jnp.mean(grad_unit * unit, axis=-1, keepdims=True))
    return scale * (grad_unit - mean_one - unit * mean_two)

def rounded_sum(terms):
    rounded = lax.optimization_barrier(terms.astype(jnp.bfloat16))
    return lax.optimization_barrier(jnp.sum(rounded.astype(jnp.float32), axis=0))

def reference(fwd_in, saved, gain, w_in, w_out, cot_in):
    results = []
    backs = []
    grads_in = []
    grads_out = []
    for s in range(N_SECTION):
        rows = fwd_in[s]
        unit, scale = normalize(rows)
        normed = (unit * gain[s]).astype(jnp.bfloat16)
        hidden = jax.nn.gelu(jnp.dot(normed, w_in[s], preferred_element_type=jnp.float32), approximate=False).astype(jnp.bfloat16)
        parts = hidden.reshape(M, N_FSDP, -1).astype(jnp.float32)
        weights = w_out[s].reshape(N_FSDP, -1, D).astype(jnp.float32)
        total = rounded_sum(jnp.einsum('mgf,gfd->gmd', parts, weights))
        results.append((rows.astype(jnp.float32) + total).astype(jnp.bfloat16))
        coming = cot_in[s]
        unit, scale = normalize(saved[s])
        normed = (unit * gain[s]).astype(jnp.bfloat16)
        pre = jnp.dot(normed, w_in[s], preferred_element_type=jnp.float32)
        hidden = jax.nn.gelu(pre, approximate=False).astype(jnp.bfloat16)
        grad_hidden = jnp.dot(coming, w_out[s].T, preferred_element_type=jnp.float32)
        grad_pre = (grad_hidden * gelu_slope(pre)).astype(jnp.bfloat16)
        parts = grad_pre.reshape(M, N_FSDP, -1).astype(jnp.float32)
        weights = w_in[s].reshape(D, N_FSDP, -1).astype(jnp.float32)
        grad_norm = rounded_sum(jnp.einsum('mgf,dgf->gmd', parts, weights))
        backs.append((coming.astype(jnp.float32) + norm_back(unit, scale, gain[s], grad_norm)).astype(jnp.bfloat16))
        grads_in.append(jnp.dot(normed.T, grad_pre, preferred_element_type=jnp.float32).astype(jnp.bfloat16))
        grads_out.append(jnp.dot(hidden.T, coming, preferred_element_type=jnp.float32).astype(jnp.bfloat16))
    empty = jnp.zeros((M, D), jnp.bfloat16)
    fwd_arrive = jnp.stack([empty] + results[:-1])
    cot_arrive = jnp.stack(backs[1:] + [empty])
    return (fwd_arrive, cot_arrive, jnp.stack(grads_in), jnp.stack(grads_out))
```

```python
import math

import jax
import jax.numpy as jnp
from jax import lax
from jax.experimental import pallas as pl
from jax.experimental.pallas import tpu as pltpu
from jax.sharding import PartitionSpec as P

MESH = pl.DeviceIdType.MESH
epsilon = 1e-06
RING = 4
PAIR = 2
UNITS = 4
ALL = slice(None)
bf16 = jnp.bfloat16
f32 = jnp.float32


def normalize(rows):
    values = rows.astype(f32)
    center = values - jnp.mean(values, axis=-1, keepdims=True)
    scale = lax.rsqrt(jnp.mean(center * center, axis=-1, keepdims=True) + epsilon)
    return (center * scale, scale)


def gelu_cdf(pre):
    return 0.5 * (1.0 + lax.erf(pre * (1.0 / math.sqrt(2.0))))


def product(left, right, dims):
    return lax.dot_general(left, right, ((dims[:1], dims[1:]), ((), ())), preferred_element_type=f32)


class Copies:
    def __init__(self, send_sem, recv_sem):
        self.send_sem, self.recv_sem, self.slots, self.sent = send_sem, recv_sem, {}, {}

    def slot(self, key):
        return self.slots.setdefault(key, len(self.slots))

    def descriptor(self, key, src, dst, device):
        i = self.slot(key)
        return pltpu.make_async_remote_copy(
            src_ref=src, dst_ref=dst, send_sem=self.send_sem.at[i], recv_sem=self.recv_sem.at[i],
            device_id=device, device_id_type=MESH,
        )

    def send(self, key, src, dst, device):
        copy = self.descriptor(key, src, dst, device)
        copy.start()
        self.sent[key] = copy

    def arrived(self, key, region, device):
        self.descriptor(key, region, region, device).wait_recv()

    def drain(self, name=None):
        for key in [k for k in self.sent if name is None or k[0] == name]:
            self.sent.pop(key).wait_send()


def body(
    fwd, saved, cot, gain, w_in, w_out,
    result, back, grad_in, grad_out,
    w1, w2, g_saved, g_cot, g_fwd, p_back, t1, t2, t3, t4, t5,
    acc, slope, hid_a, gpre, hid, totals, stage1, stage2,
    send_sem, recv_sem, load_sem, out_sem,
):
    d = fwd.shape[1]
    half = d // 2
    tile = stage1.shape[1]
    tiles = d // tile
    section, f = lax.axis_index("section"), lax.axis_index("fsdp")
    y, x, z = f // (RING * PAIR), lax.rem(f // PAIR, RING), lax.rem(f, PAIR)
    other = 1 - z

    def device(yy, xx, zz):
        return (section, (yy * RING + xx) * PAIR + zz)

    def ring(i, by):
        return lax.rem(i + by + RING, RING)

    here = {"A": (x, y), "B": (y, x)}
    near = {
        ("A", 1, 1): device(y, ring(x, 1), z), ("A", 1, -1): device(y, ring(x, -1), z),
        ("A", 3, 1): device(ring(y, 1), x, z), ("A", 3, -1): device(ring(y, -1), x, z),
    }
    for by in (1, -1):
        near["B", 1, by], near["B", 3, by] = near["A", 3, by], near["A", 1, by]
    across = device(y, x, other)

    def place(p, i1, i3, zz, cols):
        return (i3, i1, zz, ALL, cols) if p == "A" else (i1, i3, zz, ALL, cols)

    base = {"A": 0, "B": half}
    copies = Copies(send_sem, recv_sem)

    loads = [
        pltpu.make_async_copy(w_in, w1, load_sem.at[0]),
        pltpu.make_async_copy(w_out, w2, load_sem.at[1]),
    ]
    for load in loads:
        load.start()

    barrier = pltpu.get_barrier_semaphore()
    neighbours = [near["A", 1, 1], near["A", 1, -1], near["A", 3, 1], near["A", 3, -1], across]
    for neighbour in neighbours:
        pl.semaphore_signal(barrier, inc=1, device_id=neighbour, device_id_type=MESH)

    gain_row = gain[...]
    g_saved[y, x, z] = (normalize(saved[...])[0] * gain_row).astype(bf16)
    g_cot[y, x, z] = cot[...]
    g_fwd[y, x, z] = (normalize(fwd[...])[0] * gain_row).astype(bf16)
    pl.semaphore_wait(barrier, len(neighbours))

    class Gather:
        def __init__(self, name, buf):
            self.name, self.buf = name, buf

        def send(self, p, key, where, to):
            ref = self.buf.at[where]
            copies.send((self.name, p) + key, ref, ref, to)

        def wait(self, p, key, where):
            copies.arrived((self.name, p) + key, self.buf.at[where], across)

        def cols(self, p, part=None):
            if part is None:
                return pl.ds(base[p], half)
            return pl.ds(base[p] + (half // 2 if part < 0 else 0), half // 2)

        def spread(self, p, j, where):
            self.send(p, ("z", j), where, across)
            for by in (1, -1):
                self.send(p, ("long", by, j), where, near[p, 3, by])

        def start(self):
            for p in "AB":
                i1, i3 = here[p]
                own = place(p, i1, i3, z, self.cols(p))
                for by in (1, -1):
                    self.send(p, ("short", by), own, near[p, 1, by])
            for p in "AB":
                i1, i3 = here[p]
                self.spread(p, 0, place(p, i1, i3, z, self.cols(p)))

        def short_one(self):
            for p in "AB":
                i1, i3 = here[p]
                for j, by in ((1, 1), (2, -1)):
                    where = place(p, ring(i1, -by), i3, z, self.cols(p))
                    self.wait(p, ("short", by), where)
                    part = place(p, ring(i1, -by), i3, z, self.cols(p, by))
                    self.send(p, ("short2", by), part, near[p, 1, by])
                    self.spread(p, j, where)

        def short_two(self):
            for p in "AB":
                i1, i3 = here[p]
                for by in (1, -1):
                    self.wait(p, ("short2", by), place(p, ring(i1, 2), i3, z, self.cols(p, by)))
                self.spread(p, 3, place(p, ring(i1, 2), i3, z, self.cols(p)))

        def paired(self):
            for p in "AB":
                i1, i3 = here[p]
                for j, by in ((0, 0), (1, -1), (2, 1), (3, 2)):
                    self.wait(p, ("z", j), place(p, ring(i1, by), i3, other, self.cols(p)))
                for by in (1, -1):
                    self.send(p, ("longz", by), place(p, ALL, i3, other, self.cols(p)), near[p, 3, by])

        def long_one(self):
            for p in "AB":
                i1, i3 = here[p]
                for by in (1, -1):
                    for j, off in ((0, 0), (1, -1), (2, 1), (3, 2)):
                        self.wait(p, ("long", by, j), place(p, ring(i1, off), ring(i3, -by), z, self.cols(p)))
                    part = place(p, ALL, ring(i3, -by), z, self.cols(p, by))
                    self.send(p, ("long2", by), part, near[p, 3, by])

        def longz_one(self):
            for p in "AB":
                i1, i3 = here[p]
                for by in (1, -1):
                    self.wait(p, ("longz", by), place(p, ALL, ring(i3, -by), other, self.cols(p)))
                    part = place(p, ALL, ring(i3, -by), other, self.cols(p, by))
                    self.send(p, ("longz2", by), part, near[p, 3, by])

        def finish(self):
            for p in "AB":
                i1, i3 = here[p]
                for by in (1, -1):
                    self.wait(p, ("long2", by), place(p, ALL, ring(i3, 2), z, self.cols(p, by)))
                    self.wait(p, ("longz2", by), place(p, ALL, ring(i3, 2), other, self.cols(p, by)))

    width = half // UNITS

    class Scatter:
        def __init__(self, name, buf, r):
            self.name, self.buf, self.r = name, buf, r

        def cols(self, p, u, part=None):
            if part is None:
                return pl.ds(base[p] + u * width, width)
            return pl.ds(base[p] + u * width + (width // 2 if part < 0 else 0), width // 2)

        def slot(self, p, u):
            return (self.r * UNITS + u) * 2 + "AB".index(p)

        def send(self, p, u, key, where, dst, to):
            copies.send((self.name, p, u) + key, self.buf.at[where], dst, to)

        def wait(self, p, u, key, dst):
            copies.arrived((self.name, p, u) + key, dst, across)

        def add(self, where, *terms):
            if len(terms) == 1:
                self.buf[where] = self.buf[where] + terms[0][...]
            else:
                total = self.buf[where].astype(f32)
                for term in terms:
                    total += term[...].astype(f32)
                self.buf[where] = total.astype(bf16)

        def first(self, u):
            for p in "AB":
                i1, i3 = here[p]
                for k, by in enumerate((1, -1)):
                    where = place(p, ALL, ring(i3, 2), ALL, self.cols(p, u, by))
                    self.send(p, u, ("1", by), where, t1.at[self.slot(p, u), k], near[p, 3, by])

        def second(self, u):
            for p in "AB":
                i1, i3 = here[p]
                for k, by in enumerate((1, -1)):
                    slot = t1.at[self.slot(p, u), k]
                    self.wait(p, u, ("1", by), slot)
                    self.add(place(p, ALL, ring(i3, by), ALL, self.cols(p, u, by)), slot)
                    where = place(p, ALL, ring(i3, by), ALL, self.cols(p, u))
                    self.send(p, u, ("2", by), where, t2.at[self.slot(p, u), k], near[p, 3, by])

        def third(self, u):
            for p in "AB":
                i1, i3 = here[p]
                slots = [t2.at[self.slot(p, u), k] for k in range(2)]
                for k, by in enumerate((1, -1)):
                    self.wait(p, u, ("2", by), slots[k])
                self.add(place(p, ALL, i3, ALL, self.cols(p, u)), *slots)
                where = place(p, ALL, i3, other, self.cols(p, u))
                self.send(p, u, ("3",), where, t3.at[self.slot(p, u)], across)

        def fourth(self, u):
            for p in "AB":
                i1, i3 = here[p]
                slot = t3.at[self.slot(p, u)]
                self.wait(p, u, ("3",), slot)
                self.add(place(p, ALL, i3, z, self.cols(p, u)), slot)
                for k, by in enumerate((1, -1)):
                    where = place(p, ring(i1, 2), i3, z, self.cols(p, u, by))
                    self.send(p, u, ("4", by), where, t4.at[self.slot(p, u), k], near[p, 1, by])

        def fifth(self, u):
            for p in "AB":
                i1, i3 = here[p]
                for k, by in enumerate((1, -1)):
                    slot = t4.at[self.slot(p, u), k]
                    self.wait(p, u, ("4", by), slot)
                    self.add(place(p, ring(i1, by), i3, z, self.cols(p, u, by)), slot)
                    where = place(p, ring(i1, by), i3, z, self.cols(p, u))
                    self.send(p, u, ("5", by), where, t5.at[self.slot(p, u), k], near[p, 1, by])

        def last(self, u):
            for p in "AB":
                i1, i3 = here[p]
                slots = [t5.at[self.slot(p, u), k] for k in range(2)]
                for k, by in enumerate((1, -1)):
                    self.wait(p, u, ("5", by), slots[k])
                total = self.buf[place(p, i1, i3, z, self.cols(p, u))].astype(f32)
                for slot in slots:
                    total += slot[...].astype(f32)
                totals[self.r, :, self.cols(p, u)] = total

    tokens = RING * RING * PAIR * fwd.shape[0]

    def gathered(buf, cols):
        return buf[:, :, :, :, cols].reshape(tokens, tile)

    def tile_cols(k):
        return pl.ds(pl.multiple_of(k * tile, tile), tile)

    def over_features(buf, weight, dims):
        acc[...] = jnp.zeros_like(acc)

        @pl.loop(0, tiles)
        def _(k):
            cols = tile_cols(k)
            rhs = weight[cols, :] if dims == (1, 0) else weight[:, cols]
            acc[...] += product(gathered(buf, cols), rhs, dims)

    def partial_sums(buf, left, weight, dims):
        @pl.loop(0, tiles)
        def _(k):
            cols = tile_cols(k)
            rhs = weight[:, cols] if dims == (1, 0) else weight[cols, :]
            buf[:, :, :, :, cols] = product(left[...], rhs, dims).astype(bf16).reshape(buf.shape[:4] + (tile,))

    def hidden_of(dst):
        pre = acc[...]
        dst[...] = (pre * gelu_cdf(pre)).astype(bf16)

    out_copies = {}

    def grads(k):
        cols = pl.ds(k * tile, tile)
        slot = k % 2
        for which, stage in ((0, stage1), (1, stage2)):
            if (which, slot) in out_copies:
                out_copies.pop((which, slot)).wait()
            if which == 0:
                stage[slot] = product(gathered(g_saved, cols), gpre[...], (0, 0)).astype(bf16)
                dst = grad_in.at[cols, :]
            else:
                stage[slot] = product(hid_a[...], gathered(g_cot, cols), (0, 0)).astype(bf16)
                dst = grad_out.at[:, cols]
            copy = pltpu.make_async_copy(stage.at[slot], dst, out_sem.at[which, slot])
            copy.start()
            out_copies[which, slot] = copy

    a, c, n = Gather("saved", g_saved), Gather("cot", g_cot), Gather("fwd", g_fwd)
    for g in (a, c, n):
        g.start()
    a.short_one()
    a.short_two()
    c.short_one()
    c.short_two()
    a.paired()
    c.paired()
    a.long_one()
    a.longz_one()
    n.short_one()
    n.short_two()
    c.long_one()
    c.longz_one()
    a.finish()
    loads[0].wait()
    over_features(g_saved, w1, (1, 0))
    pre = acc[...]
    cdf = gelu_cdf(pre)
    hid_a[...] = (pre * cdf).astype(bf16)
    slope[...] = cdf + pre * jnp.exp(-0.5 * pre * pre) * (1.0 / math.sqrt(2.0 * math.pi))
    n.paired()
    c.finish()
    loads[1].wait()
    over_features(g_cot, w2, (1, 1))
    gpre[...] = (acc[...] * slope[...]).astype(bf16)
    n.long_one()
    partial_sums(p_back, gpre, w1, (1, 1))
    rb, rf = Scatter("back", p_back, 0), Scatter("total", g_fwd, 1)
    for u in range(UNITS):
        rb.first(u)
    n.longz_one()
    rb.second(0)
    n.finish()
    over_features(g_fwd, w1, (1, 0))
    hidden_of(hid)
    rb.second(1)
    rb.third(0)
    copies.drain("fwd")
    partial_sums(g_fwd, hid, w2, (1, 0))
    for u in range(UNITS):
        rf.first(u)
    units = [(rb, u) for u in range(UNITS)] + [(rf, u) for u in range(UNITS)]
    done = {("second", 0), ("second", 1), ("third", 0)}
    todo = list(range(tiles))
    for t in range(1, len(units) + 4):
        for lag, stage in enumerate(("second", "third", "fourth", "fifth", "last")):
            i = t - lag
            if 0 <= i < len(units) and (stage, i) not in done:
                getattr(units[i][0], stage)(units[i][1])
        for k in todo[:2]:
            grads(k)
        todo = todo[2:]

    result[...] = (fwd[...].astype(f32) + totals[1]).astype(bf16)
    unit, scale = normalize(saved[...])
    grad_unit = totals[0] * gain_row
    mean_one = jnp.mean(grad_unit, axis=-1, keepdims=True)
    mean_two = jnp.mean(grad_unit * unit, axis=-1, keepdims=True)
    back[...] = (cot[...].astype(f32) + scale * (grad_unit - mean_one - unit * mean_two)).astype(bf16)
    copies.drain()
    for copy in out_copies.values():
        copy.wait()


def tick(fwd, saved, cot, gain, w_in, w_out):
    rows, d = fwd.shape
    ff = w_in.shape[1]
    tokens = rows * RING * RING * PAIR
    tile = min(512, d // 4)
    half = d // 2
    width = half // UNITS
    slots = 2 * UNITS * 2
    gathered = pltpu.VMEM((RING, RING, PAIR, rows, d), bf16)
    vmem = pl.BlockSpec(memory_space=pltpu.VMEM)
    hbm = pl.BlockSpec(memory_space=pl.ANY)
    n_copies = 3 * 2 * 22 + 2 * UNITS * 2 * 9
    return pl.pallas_call(
        body,
        out_shape=[
            jax.ShapeDtypeStruct((rows, d), bf16),
            jax.ShapeDtypeStruct((rows, d), bf16),
            jax.ShapeDtypeStruct((d, ff), bf16),
            jax.ShapeDtypeStruct((ff, d), bf16),
        ],
        in_specs=[vmem, vmem, vmem, vmem, hbm, hbm],
        out_specs=[vmem, vmem, hbm, hbm],
        scratch_shapes=[
            pltpu.VMEM((d, ff), bf16),
            pltpu.VMEM((ff, d), bf16),
            gathered, gathered, gathered, gathered,
            pltpu.VMEM((slots, 2, RING, PAIR, rows, width // 2), bf16),
            pltpu.VMEM((slots, 2, RING, PAIR, rows, width), bf16),
            pltpu.VMEM((slots, RING, rows, width), bf16),
            pltpu.VMEM((slots, 2, rows, width // 2), bf16),
            pltpu.VMEM((slots, 2, rows, width), bf16),
            pltpu.VMEM((tokens, ff), f32),
            pltpu.VMEM((tokens, ff), f32),
            pltpu.VMEM((tokens, ff), bf16),
            pltpu.VMEM((tokens, ff), bf16),
            pltpu.VMEM((tokens, ff), bf16),
            pltpu.VMEM((2, rows, d), f32),
            pltpu.VMEM((2, tile, ff), bf16),
            pltpu.VMEM((2, ff, tile), bf16),
            pltpu.SemaphoreType.DMA((n_copies,)),
            pltpu.SemaphoreType.DMA((n_copies,)),
            pltpu.SemaphoreType.DMA((2,)),
            pltpu.SemaphoreType.DMA((2, 2)),
        ],
        compiler_params=pltpu.CompilerParams(
            collective_id=0, has_side_effects=True, vmem_limit_bytes=62 * 2**20
        ),
        cost_estimate=pl.CostEstimate(
            flops=14 * tokens * d * ff, bytes_accessed=16 * d * ff, transcendentals=3 * tokens * ff
        ),
    )(fwd, saved, cot, gain, w_in, w_out)


def passed_along(shard, axis, by):
    peers = lax.axis_size(axis)
    pairs = [(i, i + by) for i in range(peers) if 0 <= i + by < peers]
    return lax.ppermute(shard, axis, pairs)


def per_device(fwd_in, saved, gain, w_in, w_out, cot_in):
    result, back, grad_first, grad_second = tick(
        fwd_in[0], saved[0], cot_in[0], gain, w_in[0], w_out[0]
    )
    arrived = passed_along(result, "section", 1)
    returned = passed_along(back, "section", -1)
    return (arrived[None], returned[None], grad_first[None], grad_second[None])


def solution(mesh):
    return jax.shard_map(
        per_device,
        mesh=mesh,
        in_specs=(
            P("section", "fsdp", None),
            P("section", "fsdp", None),
            P("section", None),
            P("section", None, "fsdp"),
            P("section", "fsdp", None),
            P("section", "fsdp", None),
        ),
        out_specs=(
            P("section", "fsdp", None),
            P("section", "fsdp", None),
            P("section", None, "fsdp"),
            P("section", "fsdp", None),
        ),
        check_vma=False,
    )
```

```python
import math

import jax
import jax.numpy as jnp
from jax import lax
from jax.experimental import pallas as pl
from jax.experimental.pallas import tpu as pltpu
from jax.sharding import PartitionSpec as P

MESH = pl.DeviceIdType.MESH
epsilon = 1e-06
RING = 4
PAIR = 2
UNITS = 6
LATE = 512
CROSS = {"back": 0, "total": 1}
DIRECT = 3
LAGS = (0, 2, 4, 5, 6)
VMEM_MIB = 54
ALL = slice(None)
bf16 = jnp.bfloat16
f32 = jnp.float32


def normalize(rows):
    values = rows.astype(f32)
    center = values - jnp.mean(values, axis=-1, keepdims=True)
    scale = lax.rsqrt(jnp.mean(center * center, axis=-1, keepdims=True) + epsilon)
    return (center * scale, scale)


def gelu_cdf(pre):
    return 0.5 * (1.0 + lax.erf(pre * (1.0 / math.sqrt(2.0))))


def product(left, right, dims):
    return lax.dot_general(left, right, ((dims[:1], dims[1:]), ((), ())), preferred_element_type=f32)


class Copies:
    def __init__(self, send_sem, recv_sem):
        self.send_sem, self.recv_sem, self.slots, self.sent = send_sem, recv_sem, {}, {}

    def slot(self, key):
        return self.slots.setdefault(key, len(self.slots))

    def descriptor(self, key, src, dst, device):
        i = self.slot(key)
        return pltpu.make_async_remote_copy(
            src_ref=src, dst_ref=dst, send_sem=self.send_sem.at[i], recv_sem=self.recv_sem.at[i],
            device_id=device, device_id_type=MESH,
        )

    def send(self, key, src, dst, device):
        copy = self.descriptor(key, src, dst, device)
        copy.start()
        self.sent[key] = copy

    def arrived(self, key, region, device):
        self.descriptor(key, region, region, device).wait_recv()

    def drain(self, name=None):
        for key in [k for k in self.sent if name is None or k[0] == name]:
            self.sent.pop(key).wait_send()


def body(
    fwd, saved, cot, gain, w_in, w_out,
    fwd_arrive, cot_arrive, grad_in, grad_out,
    w1, w2, g_saved, g_cot, g_fwd, p_back, t0, t1, t2, t3, t4, t5,
    acc, slope, hid_a, gpre, hid, totals,
    result, back, result_in, back_in, fwd_in, last_in,
    send_sem, recv_sem, load_sem,
):
    d = fwd.shape[1]
    half = d // 2
    tile = half // UNITS
    tiles = d // tile
    section, f = lax.axis_index("section"), lax.axis_index("fsdp")
    y, x, z = f // (RING * PAIR), lax.rem(f // PAIR, RING), lax.rem(f, PAIR)
    other = 1 - z

    def device(yy, xx, zz):
        return (section, (yy * RING + xx) * PAIR + zz)

    def ring(i, by):
        return lax.rem(i + by + RING, RING)

    here = {"A": (x, y), "B": (y, x)}
    near = {
        ("A", 1, 1): device(y, ring(x, 1), z), ("A", 1, -1): device(y, ring(x, -1), z),
        ("A", 3, 1): device(ring(y, 1), x, z), ("A", 3, -1): device(ring(y, -1), x, z),
    }
    for by in (1, -1):
        near["B", 1, by], near["B", 3, by] = near["A", 3, by], near["A", 1, by]
    across = device(y, x, other)
    following = (ring(section, 1), f)
    next_at = {}
    for off in (0, 1, -1, 2):
        next_at["A", off] = (ring(section, 1), (y * RING + ring(x, off)) * PAIR + z)
        next_at["B", off] = (ring(section, 1), (ring(y, off) * RING + x) * PAIR + z)
    previous = (ring(section, -1), f)

    def place(p, i1, i3, zz, cols):
        return (i3, i1, zz, ALL, cols) if p == "A" else (i1, i3, zz, ALL, cols)

    base = {"A": 0, "B": half}
    width = half // UNITS
    copies = Copies(send_sem, recv_sem)

    loads = [
        pltpu.make_async_copy(w_in, w1, load_sem.at[0]),
        pltpu.make_async_copy(w_out, w2, load_sem.at[1]),
    ]
    for load in loads:
        load.start()

    barrier = pltpu.get_barrier_semaphore()
    neighbours = [near["A", 1, 1], near["A", 1, -1], near["A", 3, 1], near["A", 3, -1], across]
    neighbours += [following, previous]
    for by in (1, -1, 2):
        neighbours.append((ring(section, -1), (y * RING + ring(x, by)) * PAIR + z))
        neighbours.append((ring(section, -1), (ring(y, by) * RING + x) * PAIR + z))
    for neighbour in neighbours:
        pl.semaphore_signal(barrier, inc=1, device_id=neighbour, device_id_type=MESH)

    gain_row = gain[...]
    g_cot[y, x, z] = cot[...]
    pl.semaphore_wait(barrier, len(neighbours))

    class Gather:
        def __init__(self, name, buf):
            self.name, self.buf = name, buf

        def send(self, p, key, where, to):
            ref = self.buf.at[where]
            copies.send((self.name, p) + key, ref, ref, to)

        def wait(self, p, key, where):
            copies.arrived((self.name, p) + key, self.buf.at[where], across)

        def cols(self, p, part=None, span=half):
            if part is None:
                return pl.ds(base[p], span)
            return pl.ds(base[p] + (span // 2 if part < 0 else 0), span // 2)

        def early(self, p, part=None):
            return self.cols(p, part, half - LATE)

        def late(self, p):
            return pl.ds(base[p] + half - LATE, LATE)

        def spread(self, p, j, off):
            i1, i3 = here[p]
            self.send(p, ("z", j), place(p, ring(i1, off), i3, z, self.early(p)), across)
            where = place(p, ring(i1, off), i3, z, self.cols(p))
            for by in (1, -1):
                self.send(p, ("long", by, j), where, near[p, 3, by])

        def hand_over(self, p, j, off):
            if LATE == 0:
                return
            i1, i3 = here[p]
            self.send(p, ("late", j), place(p, ALL, ring(i3, off), z, self.late(p)), across)

        def start(self):
            for p in "AB":
                i1, i3 = here[p]
                own = place(p, i1, i3, z, self.cols(p))
                for by in (1, -1):
                    self.send(p, ("short", by), own, near[p, 1, by])
            for p in "AB":
                self.spread(p, 0, 0)

        def short_one(self):
            for p in "AB":
                i1, i3 = here[p]
                for j, by in ((1, 1), (2, -1)):
                    where = place(p, ring(i1, -by), i3, z, self.cols(p))
                    self.wait(p, ("short", by), where)
                    part = place(p, ring(i1, -by), i3, z, self.cols(p, by))
                    self.send(p, ("short2", by), part, near[p, 1, by])
                    self.spread(p, j, -by)

        def short_two(self):
            for p in "AB":
                i1, i3 = here[p]
                for by in (1, -1):
                    self.wait(p, ("short2", by), place(p, ring(i1, 2), i3, z, self.cols(p, by)))
                self.spread(p, 3, 2)
                self.hand_over(p, 0, 0)

        def paired(self):
            for p in "AB":
                i1, i3 = here[p]
                for j, by in ((0, 0), (1, -1), (2, 1), (3, 2)):
                    self.wait(p, ("z", j), place(p, ring(i1, by), i3, other, self.early(p)))
                for by in (1, -1):
                    self.send(p, ("longz", by), place(p, ALL, i3, other, self.early(p)), near[p, 3, by])

        def long_one(self):
            for p in "AB":
                i1, i3 = here[p]
                for by in (1, -1):
                    for j, off in ((0, 0), (1, -1), (2, 1), (3, 2)):
                        self.wait(p, ("long", by, j), place(p, ring(i1, off), ring(i3, -by), z, self.cols(p)))
                    part = place(p, ALL, ring(i3, -by), z, self.cols(p, by))
                    self.send(p, ("long2", by), part, near[p, 3, by])
                    self.hand_over(p, by, -by)

        def longz_one(self):
            for p in "AB":
                i1, i3 = here[p]
                for by in (1, -1):
                    self.wait(p, ("longz", by), place(p, ALL, ring(i3, -by), other, self.early(p)))
                    part = place(p, ALL, ring(i3, -by), other, self.early(p, by))
                    self.send(p, ("longz2", by), part, near[p, 3, by])

        def long_two(self):
            for p in "AB":
                i1, i3 = here[p]
                for by in (1, -1):
                    self.wait(p, ("long2", by), place(p, ALL, ring(i3, 2), z, self.cols(p, by)))
                self.hand_over(p, 2, 2)

        def longz_two(self):
            for p in "AB":
                i1, i3 = here[p]
                for by in (1, -1):
                    self.wait(p, ("longz2", by), place(p, ALL, ring(i3, 2), other, self.early(p, by)))

        def crossed(self):
            if LATE == 0:
                return
            for p in "AB":
                i1, i3 = here[p]
                for j, off in ((0, 0), (1, -1), (-1, 1), (2, 2)):
                    self.wait(p, ("late", j), place(p, ALL, ring(i3, off), other, self.late(p)))

    class Scatter:
        def __init__(self, name, buf, r):
            self.name, self.buf, self.r = name, buf, r
            self.cross = UNITS - CROSS[name]
            self.before = 0 if r == 0 else CROSS["back"]

        def crossing(self, p, u):
            return t0.at[self.before + u - self.cross, "AB".index(p)]

        def cols(self, p, u, part=None):
            if part is None:
                return pl.ds(base[p] + u * width, width)
            return pl.ds(base[p] + u * width + (width // 2 if part < 0 else 0), width // 2)

        def slot(self, p, u):
            return (self.r * UNITS + u) * 2 + "AB".index(p)

        def send(self, p, u, key, where, dst, to):
            copies.send((self.name, p, u) + key, self.buf.at[where], dst, to)

        def wait(self, p, u, key, dst):
            copies.arrived((self.name, p, u) + key, dst, across)

        def add(self, where, *terms):
            if len(terms) == 1:
                self.buf[where] = self.buf[where] + terms[0][...]
            else:
                total = self.buf[where].astype(f32)
                for term in terms:
                    total += term[...].astype(f32)
                self.buf[where] = total.astype(bf16)

        def depth(self, u):
            return z if u >= self.cross else ALL

        def landing(self, buf, p, u, k):
            return buf.at[self.slot(p, u), k, :, 0] if u >= self.cross else buf.at[self.slot(p, u), k]

        def zeroth(self):
            for u in range(self.cross, UNITS):
                for p in "AB":
                    where = place(p, ALL, ALL, other, self.cols(p, u))
                    self.send(p, u, ("0",), where, self.crossing(p, u), across)

        def first(self, u):
            for p in "AB":
                i1, i3 = here[p]
                if u >= self.cross:
                    slot = self.crossing(p, u)
                    self.wait(p, u, ("0",), slot)
                    self.add(place(p, ALL, ALL, z, self.cols(p, u)), slot)
                for k, by in enumerate((1, -1)):
                    where = place(p, ALL, ring(i3, 2), self.depth(u), self.cols(p, u, by))
                    self.send(p, u, ("1", by), where, self.landing(t1, p, u, k), near[p, 3, by])

        def second(self, u):
            for p in "AB":
                i1, i3 = here[p]
                for k, by in enumerate((1, -1)):
                    slot = self.landing(t1, p, u, k)
                    self.wait(p, u, ("1", by), slot)
                    self.add(place(p, ALL, ring(i3, by), self.depth(u), self.cols(p, u, by)), slot)
                    where = place(p, ALL, ring(i3, by), self.depth(u), self.cols(p, u))
                    self.send(p, u, ("2", by), where, self.landing(t2, p, u, k), near[p, 3, by])

        def third(self, u):
            for p in "AB":
                i1, i3 = here[p]
                slots = [self.landing(t2, p, u, k) for k in range(2)]
                for k, by in enumerate((1, -1)):
                    self.wait(p, u, ("2", by), slots[k])
                self.add(place(p, ALL, i3, self.depth(u), self.cols(p, u)), *slots)
                if u >= self.cross:
                    continue
                where = place(p, ALL, i3, other, self.cols(p, u))
                self.send(p, u, ("3",), where, t3.at[self.slot(p, u)], across)

        def fourth(self, u):
            for p in "AB":
                i1, i3 = here[p]
                if u < self.cross:
                    slot = t3.at[self.slot(p, u)]
                    self.wait(p, u, ("3",), slot)
                    self.add(place(p, ALL, i3, z, self.cols(p, u)), slot)
                if self.direct(u):
                    for k, off in enumerate((0, 1, -1, 2)):
                        where = place(p, ring(i1, off), i3, z, self.cols(p, u))
                        self.send(p, u, ("5", k), where, self.ending(p, u).at[k], next_at[p, off])
                    continue
                for k, by in enumerate((1, -1)):
                    where = place(p, ring(i1, 2), i3, z, self.cols(p, u, by))
                    self.send(p, u, ("4", by), where, t4.at[self.slot(p, u), k], near[p, 1, by])

        def direct(self, u):
            return self.name == "total" and u >= UNITS - DIRECT

        def ending(self, p, u):
            return last_in.at[u - (UNITS - DIRECT), "AB".index(p)]

        def fifth(self, u):
            if self.direct(u):
                return
            for p in "AB":
                i1, i3 = here[p]
                for k, by in enumerate((1, -1)):
                    slot = t4.at[self.slot(p, u), k]
                    self.wait(p, u, ("4", by), slot)
                    self.add(place(p, ring(i1, by), i3, z, self.cols(p, u, by)), slot)
                    where = place(p, ring(i1, by), i3, z, self.cols(p, u))
                    self.send(p, u, ("5", by), where, t5.at[self.slot(p, u), k], near[p, 1, by])

        def last(self, u):
            if self.direct(u):
                return
            for p in "AB":
                i1, i3 = here[p]
                slots = [t5.at[self.slot(p, u), k] for k in range(2)]
                for k, by in enumerate((1, -1)):
                    self.wait(p, u, ("5", by), slots[k])
                total = self.buf[place(p, i1, i3, z, self.cols(p, u))].astype(f32)
                for slot in slots:
                    total += slot[...].astype(f32)
                totals[self.r, :, self.cols(p, u)] = total

    tokens = RING * RING * PAIR * fwd.shape[0]

    def gathered(buf, cols):
        return buf[:, :, :, :, cols].reshape(tokens, tile)

    def tile_cols(k):
        return pl.ds(pl.multiple_of(k * tile, tile), tile)

    def over_features(buf, weight, dims, final):
        def term(k):
            cols = tile_cols(k)
            rhs = weight[cols, :] if dims == (1, 0) else weight[:, cols]
            return product(gathered(buf, cols), rhs, dims)

        if final:
            for k in (UNITS - 1, 2 * UNITS - 1):
                acc[...] += term(k)
            return
        acc[...] = term(0)

        @pl.loop(1, UNITS - 1)
        def _(k):
            acc[...] += term(k)

        @pl.loop(UNITS, 2 * UNITS - 1)
        def _(k):
            acc[...] += term(k)

    def partial_sums(buf, left, weight, dims, u):
        for p in "AB":
            cols = pl.ds(base[p] + u * width, width)
            rhs = weight[:, cols] if dims == (1, 0) else weight[cols, :]
            buf[:, :, :, :, cols] = product(left[...], rhs, dims).astype(bf16).reshape(buf.shape[:4] + (width,))

    def hidden_of(dst):
        pre = acc[...]
        dst[...] = (pre * gelu_cdf(pre)).astype(bf16)

    def grads(k):
        cols = pl.ds(k * tile, tile)
        grad_in[cols, :] = product(gathered(g_saved, cols), gpre[...], (0, 0)).astype(bf16)
        grad_out[:, cols] = product(hid_a[...], gathered(g_cot, cols), (0, 0)).astype(bf16)

    rest = DIRECT * width

    def send_result(hi):
        for p in "AB":
            cols = pl.ds(base[p], hi)
            result[:, cols] = (fwd[:, cols].astype(f32) + totals[1, :, cols]).astype(bf16)
            copies.send(("result", p), result.at[:, cols], result_in.at[:, cols], following)

    def rows_ahead(p):
        return pl.ds(base[p] + half - rest, rest), pl.ds("AB".index(p) * rest, rest)

    def send_rows():
        for p in "AB":
            mine, theirs = rows_ahead(p)
            copies.send(("rows", p), fwd.at[:, mine], fwd_in.at[:, theirs], following)

    def send_back():
        unit, scale = normalize(saved[...])
        grad_unit = totals[0] * gain_row
        mean_one = jnp.mean(grad_unit, axis=-1, keepdims=True)
        mean_two = jnp.mean(grad_unit * unit, axis=-1, keepdims=True)
        back[...] = (cot[...].astype(f32) + scale * (grad_unit - mean_one - unit * mean_two)).astype(bf16)
        copies.send(("back",), back, back_in, previous)

    a, c, n = Gather("saved", g_saved), Gather("cot", g_cot), Gather("fwd", g_fwd)
    c.start()
    g_saved[y, x, z] = (normalize(saved[...])[0] * gain_row).astype(bf16)
    a.start()
    g_fwd[y, x, z] = (normalize(fwd[...])[0] * gain_row).astype(bf16)
    n.start()
    send_rows()
    c.short_one()
    c.short_two()
    a.short_one()
    a.short_two()
    c.paired()
    a.paired()
    c.long_one()
    c.longz_one()
    a.long_one()
    a.longz_one()
    n.short_one()
    n.short_two()
    c.long_two()
    a.long_two()
    c.longz_two()
    loads[1].wait()
    over_features(g_cot, w2, (1, 1), False)
    n.paired()
    c.crossed()
    over_features(g_cot, w2, (1, 1), True)
    slope[...] = acc[...]
    a.longz_two()
    loads[0].wait()
    over_features(g_saved, w1, (1, 0), False)
    n.long_one()
    a.crossed()
    over_features(g_saved, w1, (1, 0), True)
    pre = acc[...]
    cdf = gelu_cdf(pre)
    hid_a[...] = (pre * cdf).astype(bf16)
    gelu_slope = cdf + pre * jnp.exp(-0.5 * pre * pre) * (1.0 / math.sqrt(2.0 * math.pi))
    gpre[...] = (slope[...] * gelu_slope).astype(bf16)

    rb, rf = Scatter("back", p_back, 0), Scatter("total", g_fwd, 1)
    units = [(rb, u) for u in range(UNITS)] + [(rf, u) for u in range(UNITS)]
    final = UNITS - 1

    done = set()

    def step(stage, i):
        if 0 <= i < len(units) and (stage, i) not in done:
            done.add((stage, i))
            r, u = units[i]
            getattr(r, stage)(u)

    def advance(t):
        for lag, stage in zip(LAGS, ("second", "third", "fourth", "fifth", "last")):
            step(stage, t - lag)

    def back_sums(u):
        partial_sums(p_back, gpre, w1, (1, 1), u)

    def total_sums(u):
        partial_sums(g_fwd, hid, w2, (1, 0), u)

    for u in range(rb.cross, UNITS):
        back_sums(u)
    rb.zeroth()
    for u in range(rb.cross):
        back_sums(u)
        rb.first(u)
        if u == 1:
            n.longz_one()
    n.long_two()
    advance(0)
    advance(1)
    n.longz_two()
    over_features(g_fwd, w1, (1, 0), False)
    advance(2)
    n.crossed()
    for u in range(rb.cross, UNITS):
        rb.first(u)
    over_features(g_fwd, w1, (1, 0), True)
    hidden_of(hid)
    advance(3)
    copies.drain("fwd")
    for u in range(rf.cross, UNITS):
        total_sums(u)
    rf.zeroth()
    advance(4)
    total_sums(0)
    rf.first(0)
    total_sums(1)
    rf.first(1)
    advance(5)
    for u in range(2, rf.cross):
        total_sums(u)
        rf.first(u)
    todo = list(range(tiles))
    for t in range(6, len(units) + LAGS[-1] + 1):
        if t == 2 * UNITS + 1:
            for i in (len(units) - 2, len(units) - 1):
                step("third", i)
                step("fourth", i)
        advance(t)
        if t == UNITS + 1:
            for u in range(rf.cross, UNITS):
                rf.first(u)
            copies.drain("cot")
            copies.drain("saved")
        if t == UNITS + LAGS[-1]:
            send_back()
        if t == 2 * UNITS - DIRECT - 1 + LAGS[-1]:
            send_result(half - DIRECT * width)
            copies.drain("back")
        for k in todo[:2]:
            grads(k)
        todo = todo[2:]

    copies.arrived(("back",), back_in, previous)
    cot_arrive[...] = jnp.where(section < lax.axis_size("section") - 1, back_in[...], jnp.zeros_like(back_in[...]))
    for p in "AB":
        cols = pl.ds(base[p], half - rest)
        copies.arrived(("result", p), result_in.at[:, cols], following)
        values = result_in[:, cols]
        fwd_arrive[:, cols] = jnp.where(section > 0, values, jnp.zeros_like(values))
        copies.arrived(("rows", p), fwd_in.at[:, rows_ahead(p)[1]], following)
    for u in range(UNITS - DIRECT, UNITS):
        for i, p in enumerate("AB"):
            here_in = rf.ending(p, u)
            for k in range(RING):
                copies.arrived(("total", p, u, "5", k), here_in.at[k], following)
            lo = i * rest + (u - (UNITS - DIRECT)) * width
            total = here_in[0].astype(f32)
            for k in range(1, RING):
                total += here_in[k].astype(f32)
            values = (fwd_in[:, pl.ds(lo, width)].astype(f32) + total).astype(bf16)
            fwd_arrive[:, rf.cols(p, u)] = jnp.where(section > 0, values, jnp.zeros_like(values))
    copies.drain()


def tick(fwd, saved, cot, gain, w_in, w_out):
    rows, d = fwd.shape
    ff = w_in.shape[1]
    tokens = rows * RING * RING * PAIR
    half = d // 2
    width = half // UNITS
    slots = 2 * UNITS * 2
    gathered = pltpu.VMEM((RING, RING, PAIR, rows, d), bf16)
    vmem = pl.BlockSpec(memory_space=pltpu.VMEM)
    hbm = pl.BlockSpec(memory_space=pl.ANY)
    n_copies = 3 * 2 * 26 + 2 * UNITS * 2 * 9 + 5
    return pl.pallas_call(
        body,
        out_shape=[
            pltpu.VMEM((rows, d), bf16),
            pltpu.VMEM((rows, d), bf16),
            pltpu.VMEM((d, ff), bf16),
            pltpu.VMEM((ff, d), bf16),
        ],
        in_specs=[vmem, vmem, vmem, vmem, hbm, hbm],
        out_specs=[vmem] * 4,
        scratch_shapes=[
            pltpu.VMEM((d, ff), bf16),
            pltpu.VMEM((ff, d), bf16),
            gathered, gathered, gathered, gathered,
            pltpu.VMEM((sum(CROSS.values()), 2, RING, RING, rows, width), bf16),
            pltpu.VMEM((slots, 2, RING, PAIR, rows, width // 2), bf16),
            pltpu.VMEM((slots, 2, RING, PAIR, rows, width), bf16),
            pltpu.VMEM((slots, RING, rows, width), bf16),
            pltpu.VMEM((slots, 2, rows, width // 2), bf16),
            pltpu.VMEM((slots, 2, rows, width), bf16),
            pltpu.VMEM((tokens, ff), f32),
            pltpu.VMEM((tokens, ff), f32),
            pltpu.VMEM((tokens, ff), bf16),
            pltpu.VMEM((tokens, ff), bf16),
            pltpu.VMEM((tokens, ff), bf16),
            pltpu.VMEM((2, rows, d), f32),
            *[pltpu.VMEM((rows, d), bf16)] * 4,
            pltpu.VMEM((rows, 2 * DIRECT * width), bf16),
            pltpu.VMEM((DIRECT, 2, RING, rows, width), bf16),
            pltpu.SemaphoreType.DMA((n_copies,)),
            pltpu.SemaphoreType.DMA((n_copies,)),
            pltpu.SemaphoreType.DMA((2,)),
        ],
        compiler_params=pltpu.CompilerParams(
            collective_id=0, has_side_effects=True, vmem_limit_bytes=VMEM_MIB * 2**20
        ),
        cost_estimate=pl.CostEstimate(
            flops=14 * tokens * d * ff, bytes_accessed=16 * d * ff, transcendentals=3 * tokens * ff
        ),
    )(fwd, saved, cot, gain, w_in, w_out)


def per_device(fwd_in, saved, gain, w_in, w_out, cot_in):
    outs = tick(fwd_in[0], saved[0], cot_in[0], gain, w_in[0], w_out[0])
    return tuple(out[None] for out in outs)


def solution(mesh):
    return jax.shard_map(
        per_device,
        mesh=mesh,
        in_specs=(
            P("section", "fsdp", None),
            P("section", "fsdp", None),
            P("section", None),
            P("section", None, "fsdp"),
            P("section", "fsdp", None),
            P("section", "fsdp", None),
        ),
        out_specs=(
            P("section", "fsdp", None),
            P("section", "fsdp", None),
            P("section", None, "fsdp"),
            P("section", "fsdp", None),
        ),
        check_vma=False,
    )
```

```python
import math

import jax
import jax.numpy as jnp
from jax import lax
from jax.experimental import pallas as pl
from jax.experimental.pallas import tpu as pltpu
from jax.sharding import PartitionSpec as P

MESH = pl.DeviceIdType.MESH
epsilon = 1e-06
RING = 4
PAIR = 2
UNITS = 6
LATE = 512
CROSS = {"back": 0, "total": 1}
DIRECT = 1
LAGS = (0, 2, 4, 5, 6)
TILES_A_STEP = 2
VMEM_MIB = 54
ALL = slice(None)
bf16 = jnp.bfloat16
f32 = jnp.float32


def normalize(rows):
    values = rows.astype(f32)
    center = values - jnp.mean(values, axis=-1, keepdims=True)
    scale = lax.rsqrt(jnp.mean(center * center, axis=-1, keepdims=True) + epsilon)
    return (center * scale, scale)


def gelu_cdf(pre):
    return 0.5 * (1.0 + lax.erf(pre * (1.0 / math.sqrt(2.0))))


def product(left, right, dims):
    return lax.dot_general(left, right, ((dims[:1], dims[1:]), ((), ())), preferred_element_type=f32)


class Copies:
    def __init__(self, send_sem, recv_sem):
        self.send_sem, self.recv_sem, self.slots, self.sent = send_sem, recv_sem, {}, {}

    def slot(self, key):
        return self.slots.setdefault(key, len(self.slots))

    def descriptor(self, key, src, dst, device):
        i = self.slot(key)
        return pltpu.make_async_remote_copy(
            src_ref=src, dst_ref=dst, send_sem=self.send_sem.at[i], recv_sem=self.recv_sem.at[i],
            device_id=device, device_id_type=MESH,
        )

    def send(self, key, src, dst, device):
        copy = self.descriptor(key, src, dst, device)
        copy.start()
        self.sent[key] = copy

    def arrived(self, key, region, device):
        self.descriptor(key, region, region, device).wait_recv()

    def drain(self, name=None):
        for key in [k for k in self.sent if name is None or k[0] == name]:
            self.sent.pop(key).wait_send()


def body(
    fwd_rows, saved_rows, cot_rows, gain, w_in, w_out,
    fwd_arrive, cot_arrive, grad_in, grad_out,
    w1, w2, g_saved, g_cot, g_fwd, p_back, t0, t1, t2, t3, t4, t5,
    acc, slope, hid_a, gpre, hid, totals,
    fwd, saved, cot, result, back, result_in, back_in, fwd_in, last_in,
    send_sem, recv_sem, load_sem,
):
    d = fwd_rows.shape[1]
    half = d // 2
    tile = half // UNITS
    tiles = d // tile
    section, f = lax.axis_index("section"), lax.axis_index("fsdp")
    y, x, z = f // (RING * PAIR), lax.rem(f // PAIR, RING), lax.rem(f, PAIR)
    other = 1 - z

    def device(yy, xx, zz):
        return (section, (yy * RING + xx) * PAIR + zz)

    def ring(i, by):
        return lax.rem(i + by + RING, RING)

    here = {"A": (x, y), "B": (y, x)}
    near = {
        ("A", 1, 1): device(y, ring(x, 1), z), ("A", 1, -1): device(y, ring(x, -1), z),
        ("A", 3, 1): device(ring(y, 1), x, z), ("A", 3, -1): device(ring(y, -1), x, z),
    }
    for by in (1, -1):
        near["B", 1, by], near["B", 3, by] = near["A", 3, by], near["A", 1, by]
    across = device(y, x, other)
    following = (ring(section, 1), f)
    next_at = {}
    for off in (0, 1, -1, 2):
        next_at["A", off] = (ring(section, 1), (y * RING + ring(x, off)) * PAIR + z)
        next_at["B", off] = (ring(section, 1), (ring(y, off) * RING + x) * PAIR + z)
    previous = (ring(section, -1), f)

    def place(p, i1, i3, zz, cols):
        return (i3, i1, zz, ALL, cols) if p == "A" else (i1, i3, zz, ALL, cols)

    base = {"A": 0, "B": half}
    width = half // UNITS
    copies = Copies(send_sem, recv_sem)

    barrier = pltpu.get_barrier_semaphore()
    neighbours = [near["A", 1, 1], near["A", 1, -1], near["A", 3, 1], near["A", 3, -1], across]
    neighbours += [following, previous]
    for by in (1, -1, 2):
        neighbours.append((ring(section, -1), (y * RING + ring(x, by)) * PAIR + z))
        neighbours.append((ring(section, -1), (ring(y, by) * RING + x) * PAIR + z))
    for neighbour in neighbours:
        pl.semaphore_signal(barrier, inc=1, device_id=neighbour, device_id_type=MESH)

    own = (y, x, z)
    loads = [
        pltpu.make_async_copy(source, target, load_sem.at[i])
        for i, (source, target) in enumerate(
            ((w_in, w1), (w_out, w2), (cot_rows, g_cot.at[own]), (saved_rows, saved), (fwd_rows, fwd), (cot_rows, cot))
        )
    ]
    for i in (2, 3, 4, 5, 1, 0):
        loads[i].start()

    gain_row = gain[...]
    loads[2].wait()
    pl.semaphore_wait(barrier, len(neighbours))

    class Gather:
        def __init__(self, name, buf):
            self.name, self.buf = name, buf

        def send(self, p, key, where, to):
            ref = self.buf.at[where]
            copies.send((self.name, p) + key, ref, ref, to)

        def wait(self, p, key, where):
            copies.arrived((self.name, p) + key, self.buf.at[where], across)

        def cols(self, p, part=None, span=half):
            if part is None:
                return pl.ds(base[p], span)
            return pl.ds(base[p] + (span // 2 if part < 0 else 0), span // 2)

        def early(self, p, part=None):
            return self.cols(p, part, half - LATE)

        def late(self, p):
            return pl.ds(base[p] + half - LATE, LATE)

        def spread(self, p, j, off):
            i1, i3 = here[p]
            self.send(p, ("z", j), place(p, ring(i1, off), i3, z, self.early(p)), across)
            where = place(p, ring(i1, off), i3, z, self.cols(p))
            for by in (1, -1):
                self.send(p, ("long", by, j), where, near[p, 3, by])

        def hand_over(self, p, j, off):
            if LATE == 0:
                return
            i1, i3 = here[p]
            self.send(p, ("late", j), place(p, ALL, ring(i3, off), z, self.late(p)), across)

        def start(self):
            for p in "AB":
                i1, i3 = here[p]
                own = place(p, i1, i3, z, self.cols(p))
                for by in (1, -1):
                    self.send(p, ("short", by), own, near[p, 1, by])
            for p in "AB":
                self.spread(p, 0, 0)

        def short_one(self):
            for p in "AB":
                i1, i3 = here[p]
                for j, by in ((1, 1), (2, -1)):
                    where = place(p, ring(i1, -by), i3, z, self.cols(p))
                    self.wait(p, ("short", by), where)
                    part = place(p, ring(i1, -by), i3, z, self.cols(p, by))
                    self.send(p, ("short2", by), part, near[p, 1, by])
                    self.spread(p, j, -by)

        def short_two(self):
            for p in "AB":
                i1, i3 = here[p]
                for by in (1, -1):
                    self.wait(p, ("short2", by), place(p, ring(i1, 2), i3, z, self.cols(p, by)))
                self.spread(p, 3, 2)
                self.hand_over(p, 0, 0)

        def paired(self):
            for p in "AB":
                i1, i3 = here[p]
                for j, by in ((0, 0), (1, -1), (2, 1), (3, 2)):
                    self.wait(p, ("z", j), place(p, ring(i1, by), i3, other, self.early(p)))
                for by in (1, -1):
                    self.send(p, ("longz", by), place(p, ALL, i3, other, self.early(p)), near[p, 3, by])

        def long_one(self):
            for p in "AB":
                i1, i3 = here[p]
                for by in (1, -1):
                    for j, off in ((0, 0), (1, -1), (2, 1), (3, 2)):
                        self.wait(p, ("long", by, j), place(p, ring(i1, off), ring(i3, -by), z, self.cols(p)))
                    part = place(p, ALL, ring(i3, -by), z, self.cols(p, by))
                    self.send(p, ("long2", by), part, near[p, 3, by])
                    self.hand_over(p, by, -by)

        def longz_one(self):
            for p in "AB":
                i1, i3 = here[p]
                for by in (1, -1):
                    self.wait(p, ("longz", by), place(p, ALL, ring(i3, -by), other, self.early(p)))
                    part = place(p, ALL, ring(i3, -by), other, self.early(p, by))
                    self.send(p, ("longz2", by), part, near[p, 3, by])

        def long_two(self):
            for p in "AB":
                i1, i3 = here[p]
                for by in (1, -1):
                    self.wait(p, ("long2", by), place(p, ALL, ring(i3, 2), z, self.cols(p, by)))
                self.hand_over(p, 2, 2)

        def longz_two(self):
            for p in "AB":
                i1, i3 = here[p]
                for by in (1, -1):
                    self.wait(p, ("longz2", by), place(p, ALL, ring(i3, 2), other, self.early(p, by)))

        def crossed(self):
            if LATE == 0:
                return
            for p in "AB":
                i1, i3 = here[p]
                for j, off in ((0, 0), (1, -1), (-1, 1), (2, 2)):
                    self.wait(p, ("late", j), place(p, ALL, ring(i3, off), other, self.late(p)))

    class Scatter:
        def __init__(self, name, buf, r):
            self.name, self.buf, self.r = name, buf, r
            self.cross = UNITS - CROSS[name]
            self.before = 0 if r == 0 else CROSS["back"]

        def crossing(self, p, u):
            return t0.at[self.before + u - self.cross, "AB".index(p)]

        def cols(self, p, u, part=None):
            if part is None:
                return pl.ds(base[p] + u * width, width)
            return pl.ds(base[p] + u * width + (width // 2 if part < 0 else 0), width // 2)

        def slot(self, p, u):
            return (self.r * UNITS + u) * 2 + "AB".index(p)

        def send(self, p, u, key, where, dst, to):
            copies.send((self.name, p, u) + key, self.buf.at[where], dst, to)

        def wait(self, p, u, key, dst):
            copies.arrived((self.name, p, u) + key, dst, across)

        def add(self, where, *terms):
            if len(terms) == 1:
                self.buf[where] = self.buf[where] + terms[0][...]
            else:
                total = self.buf[where].astype(f32)
                for term in terms:
                    total += term[...].astype(f32)
                self.buf[where] = total.astype(bf16)

        def depth(self, u):
            return z if u >= self.cross else ALL

        def landing(self, buf, p, u, k):
            return buf.at[self.slot(p, u), k, :, 0] if u >= self.cross else buf.at[self.slot(p, u), k]

        def zeroth(self):
            for u in range(self.cross, UNITS):
                for p in "AB":
                    where = place(p, ALL, ALL, other, self.cols(p, u))
                    self.send(p, u, ("0",), where, self.crossing(p, u), across)

        def first(self, u):
            for p in "AB":
                i1, i3 = here[p]
                if u >= self.cross:
                    slot = self.crossing(p, u)
                    self.wait(p, u, ("0",), slot)
                    self.add(place(p, ALL, ALL, z, self.cols(p, u)), slot)
                for k, by in enumerate((1, -1)):
                    where = place(p, ALL, ring(i3, 2), self.depth(u), self.cols(p, u, by))
                    self.send(p, u, ("1", by), where, self.landing(t1, p, u, k), near[p, 3, by])

        def second(self, u):
            for p in "AB":
                i1, i3 = here[p]
                for k, by in enumerate((1, -1)):
                    slot = self.landing(t1, p, u, k)
                    self.wait(p, u, ("1", by), slot)
                    self.add(place(p, ALL, ring(i3, by), self.depth(u), self.cols(p, u, by)), slot)
                    where = place(p, ALL, ring(i3, by), self.depth(u), self.cols(p, u))
                    self.send(p, u, ("2", by), where, self.landing(t2, p, u, k), near[p, 3, by])

        def third(self, u):
            for p in "AB":
                i1, i3 = here[p]
                slots = [self.landing(t2, p, u, k) for k in range(2)]
                for k, by in enumerate((1, -1)):
                    self.wait(p, u, ("2", by), slots[k])
                self.add(place(p, ALL, i3, self.depth(u), self.cols(p, u)), *slots)
                if u >= self.cross:
                    continue
                where = place(p, ALL, i3, other, self.cols(p, u))
                self.send(p, u, ("3",), where, t3.at[self.slot(p, u)], across)

        def fourth(self, u):
            for p in "AB":
                i1, i3 = here[p]
                if u < self.cross:
                    slot = t3.at[self.slot(p, u)]
                    self.wait(p, u, ("3",), slot)
                    self.add(place(p, ALL, i3, z, self.cols(p, u)), slot)
                if self.direct(u):
                    for k, off in enumerate((0, 1, -1, 2)):
                        where = place(p, ring(i1, off), i3, z, self.cols(p, u))
                        self.send(p, u, ("5", k), where, self.ending(p, u).at[k], next_at[p, off])
                    continue
                for k, by in enumerate((1, -1)):
                    where = place(p, ring(i1, 2), i3, z, self.cols(p, u, by))
                    self.send(p, u, ("4", by), where, t4.at[self.slot(p, u), k], near[p, 1, by])

        def direct(self, u):
            return self.name == "total" and u >= UNITS - DIRECT

        def ending(self, p, u):
            return last_in.at[u - (UNITS - DIRECT), "AB".index(p)]

        def fifth(self, u):
            if self.direct(u):
                return
            for p in "AB":
                i1, i3 = here[p]
                for k, by in enumerate((1, -1)):
                    slot = t4.at[self.slot(p, u), k]
                    self.wait(p, u, ("4", by), slot)
                    self.add(place(p, ring(i1, by), i3, z, self.cols(p, u, by)), slot)
                    where = place(p, ring(i1, by), i3, z, self.cols(p, u))
                    self.send(p, u, ("5", by), where, t5.at[self.slot(p, u), k], near[p, 1, by])

        def last(self, u):
            if self.direct(u):
                return
            for p in "AB":
                i1, i3 = here[p]
                slots = [t5.at[self.slot(p, u), k] for k in range(2)]
                for k, by in enumerate((1, -1)):
                    self.wait(p, u, ("5", by), slots[k])
                total = self.buf[place(p, i1, i3, z, self.cols(p, u))].astype(f32)
                for slot in slots:
                    total += slot[...].astype(f32)
                totals[self.r, :, self.cols(p, u)] = total

    tokens = RING * RING * PAIR * fwd.shape[0]

    def gathered(buf, cols):
        return buf[:, :, :, :, cols].reshape(tokens, tile)

    def tile_cols(k):
        return pl.ds(pl.multiple_of(k * tile, tile), tile)

    def over_features(buf, weight, dims, final):
        def term(k):
            cols = tile_cols(k)
            rhs = weight[cols, :] if dims == (1, 0) else weight[:, cols]
            return product(gathered(buf, cols), rhs, dims)

        if final:
            for k in (UNITS - 1, 2 * UNITS - 1):
                acc[...] += term(k)
            return
        acc[...] = term(0)

        @pl.loop(1, UNITS - 1)
        def _(k):
            acc[...] += term(k)

        @pl.loop(UNITS, 2 * UNITS - 1)
        def _(k):
            acc[...] += term(k)

    def partial_sums(buf, left, weight, dims, u):
        for p in "AB":
            cols = pl.ds(base[p] + u * width, width)
            rhs = weight[:, cols] if dims == (1, 0) else weight[cols, :]
            buf[:, :, :, :, cols] = product(left[...], rhs, dims).astype(bf16).reshape(buf.shape[:4] + (width,))

    def hidden_of(dst):
        pre = acc[...]
        dst[...] = (pre * gelu_cdf(pre)).astype(bf16)

    def grads(k):
        cols = pl.ds(k * tile, tile)
        grad_in[cols, :] = product(gathered(g_saved, cols), gpre[...], (0, 0)).astype(bf16)
        grad_out[:, cols] = product(hid_a[...], gathered(g_cot, cols), (0, 0)).astype(bf16)

    rest = DIRECT * width

    def send_result(hi):
        for p in "AB":
            cols = pl.ds(base[p], hi)
            result[:, cols] = (fwd[:, cols].astype(f32) + totals[1, :, cols]).astype(bf16)
            copies.send(("result", p), result.at[:, cols], result_in.at[:, cols], following)

    def rows_ahead(p):
        return pl.ds(base[p] + half - rest, rest), pl.ds("AB".index(p) * rest, rest)

    def send_rows():
        for p in "AB":
            mine, theirs = rows_ahead(p)
            copies.send(("rows", p), fwd.at[:, mine], fwd_in.at[:, theirs], following)

    def send_back():
        unit, scale = normalize(saved[...])
        grad_unit = totals[0] * gain_row
        mean_one = jnp.mean(grad_unit, axis=-1, keepdims=True)
        mean_two = jnp.mean(grad_unit * unit, axis=-1, keepdims=True)
        back[...] = (cot[...].astype(f32) + scale * (grad_unit - mean_one - unit * mean_two)).astype(bf16)
        copies.send(("back",), back, back_in, previous)

    a, c, n = Gather("saved", g_saved), Gather("cot", g_cot), Gather("fwd", g_fwd)
    c.start()
    loads[3].wait()
    g_saved[y, x, z] = (normalize(saved[...])[0] * gain_row).astype(bf16)
    a.start()
    loads[4].wait()
    g_fwd[y, x, z] = (normalize(fwd[...])[0] * gain_row).astype(bf16)
    n.start()
    send_rows()
    loads[5].wait()
    c.short_one()
    c.short_two()
    a.short_one()
    a.short_two()
    c.paired()
    a.paired()
    c.long_one()
    c.longz_one()
    a.long_one()
    a.longz_one()
    n.short_one()
    n.short_two()
    c.long_two()
    a.long_two()
    c.longz_two()
    loads[1].wait()
    over_features(g_cot, w2, (1, 1), False)
    n.paired()
    c.crossed()
    over_features(g_cot, w2, (1, 1), True)
    slope[...] = acc[...]
    a.longz_two()
    loads[0].wait()
    over_features(g_saved, w1, (1, 0), False)
    n.long_one()
    a.crossed()
    over_features(g_saved, w1, (1, 0), True)
    pre = acc[...]
    cdf = gelu_cdf(pre)
    hid_a[...] = (pre * cdf).astype(bf16)
    gelu_slope = cdf + pre * jnp.exp(-0.5 * pre * pre) * (1.0 / math.sqrt(2.0 * math.pi))
    gpre[...] = (slope[...] * gelu_slope).astype(bf16)

    rb, rf = Scatter("back", p_back, 0), Scatter("total", g_fwd, 1)
    units = [(rb, u) for u in range(UNITS)] + [(rf, u) for u in range(UNITS)]
    final = UNITS - 1

    done = set()

    def step(stage, i):
        if 0 <= i < len(units) and (stage, i) not in done:
            done.add((stage, i))
            r, u = units[i]
            getattr(r, stage)(u)

    def advance(t):
        for lag, stage in zip(LAGS, ("second", "third", "fourth", "fifth", "last")):
            step(stage, t - lag)

    def back_sums(u):
        partial_sums(p_back, gpre, w1, (1, 1), u)

    def total_sums(u):
        partial_sums(g_fwd, hid, w2, (1, 0), u)

    for u in range(rb.cross, UNITS):
        back_sums(u)
    rb.zeroth()
    for u in range(rb.cross):
        back_sums(u)
        rb.first(u)
        if u == 1:
            n.longz_one()
    n.long_two()
    advance(0)
    advance(1)
    n.longz_two()
    over_features(g_fwd, w1, (1, 0), False)
    advance(2)
    n.crossed()
    for u in range(rb.cross, UNITS):
        rb.first(u)
    over_features(g_fwd, w1, (1, 0), True)
    hidden_of(hid)
    advance(3)
    copies.drain("fwd")
    for u in range(rf.cross, UNITS):
        total_sums(u)
    rf.zeroth()
    for t in range(4, UNITS):
        advance(t)
        total_sums(t - 4)
        rf.first(t - 4)
    for u in range(UNITS - 4, rf.cross):
        total_sums(u)
        rf.first(u)
    todo = list(range(tiles))
    for t in range(UNITS, len(units) + LAGS[-1] + 1):
        if t == 2 * UNITS + 1:
            for i in (len(units) - 2, len(units) - 1):
                step("third", i)
                step("fourth", i)
        advance(t)
        if t == 2 * UNITS - 3:
            for u in range(rf.cross, UNITS):
                rf.first(u)
        if t == UNITS + 1:
            copies.drain("cot")
            copies.drain("saved")
        if t == UNITS + LAGS[-1]:
            send_back()
        if t == 2 * UNITS - DIRECT - 1 + LAGS[-1]:
            send_result(half - DIRECT * width)
            copies.drain("back")
        for k in todo[:TILES_A_STEP]:
            grads(k)
        todo = todo[TILES_A_STEP:]

    copies.drain()
    copies.arrived(("back",), back_in, previous)
    cot_arrive[...] = jnp.where(section < lax.axis_size("section") - 1, back_in[...], jnp.zeros_like(back_in[...]))
    for p in "AB":
        cols = pl.ds(base[p], half - rest)
        copies.arrived(("result", p), result_in.at[:, cols], following)
        values = result_in[:, cols]
        fwd_arrive[:, cols] = jnp.where(section > 0, values, jnp.zeros_like(values))
        copies.arrived(("rows", p), fwd_in.at[:, rows_ahead(p)[1]], following)
    for u in range(UNITS - DIRECT, UNITS):
        for i, p in enumerate("AB"):
            here_in = rf.ending(p, u)
            for k in range(RING):
                copies.arrived(("total", p, u, "5", k), here_in.at[k], following)
            lo = i * rest + (u - (UNITS - DIRECT)) * width
            total = here_in[0].astype(f32)
            for k in range(1, RING):
                total += here_in[k].astype(f32)
            values = (fwd_in[:, pl.ds(lo, width)].astype(f32) + total).astype(bf16)
            fwd_arrive[:, rf.cols(p, u)] = jnp.where(section > 0, values, jnp.zeros_like(values))


def tick(fwd, saved, cot, gain, w_in, w_out):
    rows, d = fwd.shape
    ff = w_in.shape[1]
    tokens = rows * RING * RING * PAIR
    half = d // 2
    width = half // UNITS
    slots = 2 * UNITS * 2
    gathered = pltpu.VMEM((RING, RING, PAIR, rows, d), bf16)
    vmem = pl.BlockSpec(memory_space=pltpu.VMEM)
    hbm = pl.BlockSpec(memory_space=pl.ANY)
    n_copies = 3 * 2 * 26 + 2 * UNITS * 2 * 9 + 5
    return pl.pallas_call(
        body,
        out_shape=[
            pltpu.VMEM((rows, d), bf16),
            pltpu.VMEM((rows, d), bf16),
            pltpu.VMEM((d, ff), bf16),
            pltpu.VMEM((ff, d), bf16),
        ],
        in_specs=[hbm, hbm, hbm, vmem, hbm, hbm],
        out_specs=[vmem] * 4,
        scratch_shapes=[
            pltpu.VMEM((d, ff), bf16),
            pltpu.VMEM((ff, d), bf16),
            gathered, gathered, gathered, gathered,
            pltpu.VMEM((sum(CROSS.values()), 2, RING, RING, rows, width), bf16),
            pltpu.VMEM((slots, 2, RING, PAIR, rows, width // 2), bf16),
            pltpu.VMEM((slots, 2, RING, PAIR, rows, width), bf16),
            pltpu.VMEM((slots, RING, rows, width), bf16),
            pltpu.VMEM((slots, 2, rows, width // 2), bf16),
            pltpu.VMEM((slots, 2, rows, width), bf16),
            pltpu.VMEM((tokens, ff), f32),
            pltpu.VMEM((tokens, ff), f32),
            pltpu.VMEM((tokens, ff), bf16),
            pltpu.VMEM((tokens, ff), bf16),
            pltpu.VMEM((tokens, ff), bf16),
            pltpu.VMEM((2, rows, d), f32),
            *[pltpu.VMEM((rows, d), bf16)] * 7,
            pltpu.VMEM((rows, 2 * DIRECT * width), bf16),
            pltpu.VMEM((DIRECT, 2, RING, rows, width), bf16),
            pltpu.SemaphoreType.DMA((n_copies,)),
            pltpu.SemaphoreType.DMA((n_copies,)),
            pltpu.SemaphoreType.DMA((6,)),
        ],
        compiler_params=pltpu.CompilerParams(
            collective_id=0, has_side_effects=True, vmem_limit_bytes=VMEM_MIB * 2**20
        ),
        cost_estimate=pl.CostEstimate(
            flops=14 * tokens * d * ff, bytes_accessed=16 * d * ff, transcendentals=3 * tokens * ff
        ),
    )(fwd, saved, cot, gain, w_in, w_out)


def move(*refs):
    sources, targets, sem = refs[:4], refs[4:8], refs[8]
    copies = [pltpu.make_async_copy(s, t, sem.at[i]) for i, (s, t) in enumerate(zip(sources, targets))]
    for copy in copies:
        copy.start()
    for copy in copies:
        copy.wait()


def placed(*arrays):
    hbm = pl.BlockSpec(memory_space=pl.ANY)
    return pl.pallas_call(
        move,
        out_shape=[pltpu.HBM(a.shape, a.dtype) for a in arrays],
        in_specs=[hbm] * 4,
        out_specs=[hbm] * 4,
        scratch_shapes=[pltpu.SemaphoreType.DMA((4,))],
        compiler_params=pltpu.CompilerParams(vmem_limit_bytes=2 * 2**20),
    )(*arrays)


def per_device(fwd_in, saved, gain, w_in, w_out, cot_in):
    outs = tick(fwd_in[0], saved[0], cot_in[0], gain, w_in[0], w_out[0])
    return tuple(out[None] for out in placed(*outs))


def solution(mesh):
    return jax.shard_map(
        per_device,
        mesh=mesh,
        in_specs=(
            P("section", "fsdp", None),
            P("section", "fsdp", None),
            P("section", None),
            P("section", None, "fsdp"),
            P("section", "fsdp", None),
            P("section", "fsdp", None),
        ),
        out_specs=(
            P("section", "fsdp", None),
            P("section", "fsdp", None),
            P("section", None, "fsdp"),
            P("section", "fsdp", None),
        ),
        check_vma=False,
    )
```

```python
import math

import jax
import jax.numpy as jnp
from jax import lax
from jax.experimental import pallas as pl
from jax.experimental.pallas import tpu as pltpu
from jax.sharding import PartitionSpec as P

MESH = pl.DeviceIdType.MESH
epsilon = 1e-06
RING = 4
PAIR = 2
UNITS = 6
LATE = 512
CROSS = {"back": 0, "total": 1}
DIRECT = 1
LAGS = (0, 2, 4, 5, 6)
VMEM_MIB = 54
ALL = slice(None)
bf16 = jnp.bfloat16
f32 = jnp.float32


def normalize(rows):
    values = rows.astype(f32)
    center = values - jnp.mean(values, axis=-1, keepdims=True)
    scale = lax.rsqrt(jnp.mean(center * center, axis=-1, keepdims=True) + epsilon)
    return (center * scale, scale)


def gelu_cdf(pre):
    return 0.5 * (1.0 + lax.erf(pre * (1.0 / math.sqrt(2.0))))


def product(left, right, dims):
    return lax.dot_general(left, right, ((dims[:1], dims[1:]), ((), ())), preferred_element_type=f32)


class Copies:
    def __init__(self, send_sem, recv_sem):
        self.send_sem, self.recv_sem, self.slots, self.sent = send_sem, recv_sem, {}, {}

    def slot(self, key):
        return self.slots.setdefault(key, len(self.slots))

    def descriptor(self, key, src, dst, device):
        i = self.slot(key)
        return pltpu.make_async_remote_copy(
            src_ref=src, dst_ref=dst, send_sem=self.send_sem.at[i], recv_sem=self.recv_sem.at[i],
            device_id=device, device_id_type=MESH,
        )

    def send(self, key, src, dst, device):
        copy = self.descriptor(key, src, dst, device)
        copy.start()
        self.sent[key] = copy

    def arrived(self, key, region, device):
        self.descriptor(key, region, region, device).wait_recv()

    def drain(self, name=None):
        for key in [k for k in self.sent if name is None or k[0] == name]:
            self.sent.pop(key).wait_send()


def body(
    fwd_rows, saved_rows, cot_rows, gain, w_in, w_out,
    fwd_arrive, cot_arrive, grad_in, grad_out,
    w1, w2, g_saved, g_cot, g_fwd, p_back, t0, t1, t2, t3, t4, t5,
    acc, slope, hid_a, gpre, hid, totals,
    fwd, saved, cot, result, back, result_in, back_in, fwd_in, last_in,
    send_sem, recv_sem, load_sem,
):
    d = fwd_rows.shape[1]
    half = d // 2
    tile = half // UNITS
    tiles = d // tile
    section, f = lax.axis_index("section"), lax.axis_index("fsdp")
    y, x, z = f // (RING * PAIR), lax.rem(f // PAIR, RING), lax.rem(f, PAIR)
    other = 1 - z

    def device(yy, xx, zz):
        return (section, (yy * RING + xx) * PAIR + zz)

    def ring(i, by):
        return lax.rem(i + by + RING, RING)

    here = {"A": (x, y), "B": (y, x)}
    near = {
        ("A", 1, 1): device(y, ring(x, 1), z), ("A", 1, -1): device(y, ring(x, -1), z),
        ("A", 3, 1): device(ring(y, 1), x, z), ("A", 3, -1): device(ring(y, -1), x, z),
    }
    for by in (1, -1):
        near["B", 1, by], near["B", 3, by] = near["A", 3, by], near["A", 1, by]
    across = device(y, x, other)
    following = (ring(section, 1), f)
    next_at = {}
    for off in (0, 1, -1, 2):
        next_at["A", off] = (ring(section, 1), (y * RING + ring(x, off)) * PAIR + z)
        next_at["B", off] = (ring(section, 1), (ring(y, off) * RING + x) * PAIR + z)
    previous = (ring(section, -1), f)

    def place(p, i1, i3, zz, cols):
        return (i3, i1, zz, ALL, cols) if p == "A" else (i1, i3, zz, ALL, cols)

    base = {"A": 0, "B": half}
    width = half // UNITS
    copies = Copies(send_sem, recv_sem)

    barrier = pltpu.get_barrier_semaphore()
    neighbours = [near["A", 1, 1], near["A", 1, -1], near["A", 3, 1], near["A", 3, -1], across]
    neighbours += [following, previous]
    for by in (1, -1, 2):
        neighbours.append((ring(section, -1), (y * RING + ring(x, by)) * PAIR + z))
        neighbours.append((ring(section, -1), (ring(y, by) * RING + x) * PAIR + z))
    for neighbour in neighbours:
        pl.semaphore_signal(barrier, inc=1, device_id=neighbour, device_id_type=MESH)

    own = (y, x, z)
    loads = [
        pltpu.make_async_copy(source, target, load_sem.at[i])
        for i, (source, target) in enumerate(
            ((w_in, w1), (w_out, w2), (cot_rows, g_cot.at[own]), (saved_rows, saved), (fwd_rows, fwd), (cot_rows, cot))
        )
    ]
    for i in (2, 3, 4, 5, 1, 0):
        loads[i].start()

    gain_row = gain[...]
    loads[2].wait()
    pl.semaphore_wait(barrier, len(neighbours))

    class Gather:
        def __init__(self, name, buf):
            self.name, self.buf = name, buf

        def send(self, p, key, where, to):
            ref = self.buf.at[where]
            copies.send((self.name, p) + key, ref, ref, to)

        def wait(self, p, key, where):
            copies.arrived((self.name, p) + key, self.buf.at[where], across)

        def cols(self, p, part=None, span=half):
            if part is None:
                return pl.ds(base[p], span)
            return pl.ds(base[p] + (span // 2 if part < 0 else 0), span // 2)

        def early(self, p, part=None):
            return self.cols(p, part, half - LATE)

        def late(self, p):
            return pl.ds(base[p] + half - LATE, LATE)

        def spread(self, p, j, off):
            i1, i3 = here[p]
            self.send(p, ("z", j), place(p, ring(i1, off), i3, z, self.early(p)), across)
            where = place(p, ring(i1, off), i3, z, self.cols(p))
            for by in (1, -1):
                self.send(p, ("long", by, j), where, near[p, 3, by])

        def hand_over(self, p, j, off):
            if LATE == 0:
                return
            i1, i3 = here[p]
            self.send(p, ("late", j), place(p, ALL, ring(i3, off), z, self.late(p)), across)

        def start(self):
            for p in "AB":
                i1, i3 = here[p]
                own = place(p, i1, i3, z, self.cols(p))
                for by in (1, -1):
                    self.send(p, ("short", by), own, near[p, 1, by])
            for p in "AB":
                self.spread(p, 0, 0)

        def short_one(self):
            for p in "AB":
                i1, i3 = here[p]
                for j, by in ((1, 1), (2, -1)):
                    where = place(p, ring(i1, -by), i3, z, self.cols(p))
                    self.wait(p, ("short", by), where)
                    part = place(p, ring(i1, -by), i3, z, self.cols(p, by))
                    self.send(p, ("short2", by), part, near[p, 1, by])
                    self.spread(p, j, -by)

        def short_two(self):
            for p in "AB":
                i1, i3 = here[p]
                for by in (1, -1):
                    self.wait(p, ("short2", by), place(p, ring(i1, 2), i3, z, self.cols(p, by)))
                self.spread(p, 3, 2)
                self.hand_over(p, 0, 0)

        def paired(self):
            for p in "AB":
                i1, i3 = here[p]
                for j, by in ((0, 0), (1, -1), (2, 1), (3, 2)):
                    self.wait(p, ("z", j), place(p, ring(i1, by), i3, other, self.early(p)))
                for by in (1, -1):
                    self.send(p, ("longz", by), place(p, ALL, i3, other, self.early(p)), near[p, 3, by])

        def long_one(self):
            for p in "AB":
                i1, i3 = here[p]
                for by in (1, -1):
                    for j, off in ((0, 0), (1, -1), (2, 1), (3, 2)):
                        self.wait(p, ("long", by, j), place(p, ring(i1, off), ring(i3, -by), z, self.cols(p)))
                    part = place(p, ALL, ring(i3, -by), z, self.cols(p, by))
                    self.send(p, ("long2", by), part, near[p, 3, by])
                    self.hand_over(p, by, -by)

        def longz_one(self):
            for p in "AB":
                i1, i3 = here[p]
                for by in (1, -1):
                    self.wait(p, ("longz", by), place(p, ALL, ring(i3, -by), other, self.early(p)))
                    part = place(p, ALL, ring(i3, -by), other, self.early(p, by))
                    self.send(p, ("longz2", by), part, near[p, 3, by])

        def long_two(self):
            for p in "AB":
                i1, i3 = here[p]
                for by in (1, -1):
                    self.wait(p, ("long2", by), place(p, ALL, ring(i3, 2), z, self.cols(p, by)))
                self.hand_over(p, 2, 2)

        def longz_two(self):
            for p in "AB":
                i1, i3 = here[p]
                for by in (1, -1):
                    self.wait(p, ("longz2", by), place(p, ALL, ring(i3, 2), other, self.early(p, by)))

        def crossed(self):
            if LATE == 0:
                return
            for p in "AB":
                i1, i3 = here[p]
                for j, off in ((0, 0), (1, -1), (-1, 1), (2, 2)):
                    self.wait(p, ("late", j), place(p, ALL, ring(i3, off), other, self.late(p)))

    class Scatter:
        def __init__(self, name, buf, r):
            self.name, self.buf, self.r = name, buf, r
            self.cross = UNITS - CROSS[name]
            self.before = 0 if r == 0 else CROSS["back"]

        def crossing(self, p, u):
            return t0.at[self.before + u - self.cross, "AB".index(p)]

        def cols(self, p, u, part=None):
            if part is None:
                return pl.ds(base[p] + u * width, width)
            return pl.ds(base[p] + u * width + (width // 2 if part < 0 else 0), width // 2)

        def slot(self, p, u):
            return (self.r * UNITS + u) * 2 + "AB".index(p)

        def send(self, p, u, key, where, dst, to):
            copies.send((self.name, p, u) + key, self.buf.at[where], dst, to)

        def wait(self, p, u, key, dst):
            copies.arrived((self.name, p, u) + key, dst, across)

        def add(self, where, *terms):
            if len(terms) == 1:
                self.buf[where] = self.buf[where] + terms[0][...]
            else:
                total = self.buf[where].astype(f32)
                for term in terms:
                    total += term[...].astype(f32)
                self.buf[where] = total.astype(bf16)

        def depth(self, u):
            return z if u >= self.cross else ALL

        def landing(self, buf, p, u, k):
            return buf.at[self.slot(p, u), k, :, 0] if u >= self.cross else buf.at[self.slot(p, u), k]

        def zeroth(self):
            for u in range(self.cross, UNITS):
                for p in "AB":
                    where = place(p, ALL, ALL, other, self.cols(p, u))
                    self.send(p, u, ("0",), where, self.crossing(p, u), across)

        def first(self, u):
            for p in "AB":
                i1, i3 = here[p]
                if u >= self.cross:
                    slot = self.crossing(p, u)
                    self.wait(p, u, ("0",), slot)
                    self.add(place(p, ALL, ALL, z, self.cols(p, u)), slot)
                for k, by in enumerate((1, -1)):
                    where = place(p, ALL, ring(i3, 2), self.depth(u), self.cols(p, u, by))
                    self.send(p, u, ("1", by), where, self.landing(t1, p, u, k), near[p, 3, by])

        def second(self, u):
            for p in "AB":
                i1, i3 = here[p]
                for k, by in enumerate((1, -1)):
                    slot = self.landing(t1, p, u, k)
                    self.wait(p, u, ("1", by), slot)
                    self.add(place(p, ALL, ring(i3, by), self.depth(u), self.cols(p, u, by)), slot)
                    where = place(p, ALL, ring(i3, by), self.depth(u), self.cols(p, u))
                    self.send(p, u, ("2", by), where, self.landing(t2, p, u, k), near[p, 3, by])

        def third(self, u):
            for p in "AB":
                i1, i3 = here[p]
                slots = [self.landing(t2, p, u, k) for k in range(2)]
                for k, by in enumerate((1, -1)):
                    self.wait(p, u, ("2", by), slots[k])
                self.add(place(p, ALL, i3, self.depth(u), self.cols(p, u)), *slots)
                if u >= self.cross:
                    continue
                where = place(p, ALL, i3, other, self.cols(p, u))
                self.send(p, u, ("3",), where, t3.at[self.slot(p, u)], across)

        def fourth(self, u):
            for p in "AB":
                i1, i3 = here[p]
                if u < self.cross:
                    slot = t3.at[self.slot(p, u)]
                    self.wait(p, u, ("3",), slot)
                    self.add(place(p, ALL, i3, z, self.cols(p, u)), slot)
                if self.direct(u):
                    for k, off in enumerate((0, 1, -1, 2)):
                        where = place(p, ring(i1, off), i3, z, self.cols(p, u))
                        self.send(p, u, ("5", k), where, self.ending(p, u).at[k], next_at[p, off])
                    continue
                for k, by in enumerate((1, -1)):
                    where = place(p, ring(i1, 2), i3, z, self.cols(p, u, by))
                    self.send(p, u, ("4", by), where, t4.at[self.slot(p, u), k], near[p, 1, by])

        def direct(self, u):
            return self.name == "total" and u >= UNITS - DIRECT

        def ending(self, p, u):
            return last_in.at[u - (UNITS - DIRECT), "AB".index(p)]

        def fifth(self, u):
            if self.direct(u):
                return
            for p in "AB":
                i1, i3 = here[p]
                for k, by in enumerate((1, -1)):
                    slot = t4.at[self.slot(p, u), k]
                    self.wait(p, u, ("4", by), slot)
                    self.add(place(p, ring(i1, by), i3, z, self.cols(p, u, by)), slot)
                    where = place(p, ring(i1, by), i3, z, self.cols(p, u))
                    self.send(p, u, ("5", by), where, t5.at[self.slot(p, u), k], near[p, 1, by])

        def last(self, u):
            if self.direct(u):
                return
            for p in "AB":
                i1, i3 = here[p]
                slots = [t5.at[self.slot(p, u), k] for k in range(2)]
                for k, by in enumerate((1, -1)):
                    self.wait(p, u, ("5", by), slots[k])
                total = self.buf[place(p, i1, i3, z, self.cols(p, u))].astype(f32)
                for slot in slots:
                    total += slot[...].astype(f32)
                totals[self.r, :, self.cols(p, u)] = total

    tokens = RING * RING * PAIR * fwd.shape[0]

    def gathered(buf, cols):
        return buf[:, :, :, :, cols].reshape(tokens, tile)

    def tile_cols(k):
        return pl.ds(pl.multiple_of(k * tile, tile), tile)

    def over_features(buf, weight, dims, final):
        def term(k):
            cols = tile_cols(k)
            rhs = weight[cols, :] if dims == (1, 0) else weight[:, cols]
            return product(gathered(buf, cols), rhs, dims)

        if final:
            for k in (UNITS - 1, 2 * UNITS - 1):
                acc[...] += term(k)
            return
        acc[...] = term(0)

        @pl.loop(1, UNITS - 1)
        def _(k):
            acc[...] += term(k)

        @pl.loop(UNITS, 2 * UNITS - 1)
        def _(k):
            acc[...] += term(k)

    def partial_sums(buf, left, weight, dims, u):
        for p in "AB":
            cols = pl.ds(base[p] + u * width, width)
            rhs = weight[:, cols] if dims == (1, 0) else weight[cols, :]
            buf[:, :, :, :, cols] = product(left[...], rhs, dims).astype(bf16).reshape(buf.shape[:4] + (width,))

    def hidden_of(dst):
        pre = acc[...]
        dst[...] = (pre * gelu_cdf(pre)).astype(bf16)

    def grads(k):
        cols = pl.ds(k * tile, tile)
        grad_in[cols, :] = product(gathered(g_saved, cols), gpre[...], (0, 0)).astype(bf16)
        grad_out[:, cols] = product(hid_a[...], gathered(g_cot, cols), (0, 0)).astype(bf16)

    rest = DIRECT * width

    def send_result(hi):
        for p in "AB":
            cols = pl.ds(base[p], hi)
            result[:, cols] = (fwd[:, cols].astype(f32) + totals[1, :, cols]).astype(bf16)
            copies.send(("result", p), result.at[:, cols], result_in.at[:, cols], following)

    def rows_ahead(p):
        return pl.ds(base[p] + half - rest, rest), pl.ds("AB".index(p) * rest, rest)

    def send_rows():
        for p in "AB":
            mine, theirs = rows_ahead(p)
            copies.send(("rows", p), fwd.at[:, mine], fwd_in.at[:, theirs], following)

    def send_back():
        unit, scale = normalize(saved[...])
        grad_unit = totals[0] * gain_row
        mean_one = jnp.mean(grad_unit, axis=-1, keepdims=True)
        mean_two = jnp.mean(grad_unit * unit, axis=-1, keepdims=True)
        back[...] = (cot[...].astype(f32) + scale * (grad_unit - mean_one - unit * mean_two)).astype(bf16)
        copies.send(("back",), back, back_in, previous)

    a, c, n = Gather("saved", g_saved), Gather("cot", g_cot), Gather("fwd", g_fwd)
    c.start()
    loads[3].wait()
    g_saved[y, x, z] = (normalize(saved[...])[0] * gain_row).astype(bf16)
    a.start()
    loads[4].wait()
    g_fwd[y, x, z] = (normalize(fwd[...])[0] * gain_row).astype(bf16)
    n.start()
    send_rows()
    loads[5].wait()
    c.short_one()
    c.short_two()
    a.short_one()
    a.short_two()
    c.paired()
    a.paired()
    c.long_one()
    c.longz_one()
    a.long_one()
    a.longz_one()
    n.short_one()
    n.short_two()
    c.long_two()
    a.long_two()
    c.longz_two()
    loads[1].wait()
    over_features(g_cot, w2, (1, 1), False)
    n.paired()
    c.crossed()
    over_features(g_cot, w2, (1, 1), True)
    slope[...] = acc[...]
    a.longz_two()
    loads[0].wait()
    over_features(g_saved, w1, (1, 0), False)
    n.long_one()
    a.crossed()
    over_features(g_saved, w1, (1, 0), True)
    pre = acc[...]
    cdf = gelu_cdf(pre)
    hid_a[...] = (pre * cdf).astype(bf16)
    gelu_slope = cdf + pre * jnp.exp(-0.5 * pre * pre) * (1.0 / math.sqrt(2.0 * math.pi))
    gpre[...] = (slope[...] * gelu_slope).astype(bf16)

    rb, rf = Scatter("back", p_back, 0), Scatter("total", g_fwd, 1)
    units = [(rb, u) for u in range(UNITS)] + [(rf, u) for u in range(UNITS)]
    final = UNITS - 1

    done = set()

    def step(stage, i):
        if 0 <= i < len(units) and (stage, i) not in done:
            done.add((stage, i))
            r, u = units[i]
            getattr(r, stage)(u)

    def advance(t):
        for lag, stage in zip(LAGS, ("second", "third", "fourth", "fifth", "last")):
            step(stage, t - lag)

    def back_sums(u):
        partial_sums(p_back, gpre, w1, (1, 1), u)

    def total_sums(u):
        partial_sums(g_fwd, hid, w2, (1, 0), u)

    for u in range(rb.cross, UNITS):
        back_sums(u)
    rb.zeroth()
    for u in range(rb.cross):
        back_sums(u)
        rb.first(u)
        if u == 1:
            n.longz_one()
    n.long_two()
    todo = list(range(tiles))

    def some_grads(count):
        for _ in range(min(count, len(todo))):
            grads(todo.pop(0))

    advance(0)
    some_grads(2)
    advance(1)
    some_grads(1)
    n.longz_two()
    over_features(g_fwd, w1, (1, 0), False)
    advance(2)
    some_grads(1)
    n.crossed()
    for u in range(rb.cross, UNITS):
        rb.first(u)
    over_features(g_fwd, w1, (1, 0), True)
    hidden_of(hid)
    advance(3)
    copies.drain("fwd")
    for u in range(rf.cross, UNITS):
        total_sums(u)
    rf.zeroth()
    for t in range(4, UNITS):
        advance(t)
        total_sums(t - 4)
        rf.first(t - 4)
    for u in range(UNITS - 4, rf.cross):
        total_sums(u)
        rf.first(u)
    for t in range(UNITS, len(units) + LAGS[-1] + 1):
        if t == 2 * UNITS + 1:
            for i in (len(units) - 2, len(units) - 1):
                step("third", i)
                step("fourth", i)
        advance(t)
        if t == 2 * UNITS - 3:
            for u in range(rf.cross, UNITS):
                rf.first(u)
        if t == UNITS + 1:
            copies.drain("cot")
            copies.drain("saved")
        if t == UNITS + LAGS[-1]:
            send_back()
        if t == 2 * UNITS - DIRECT - 1 + LAGS[-1]:
            send_result(half - DIRECT * width)
            copies.drain("back")
        some_grads(2 if t < UNITS + 2 else 1)

    copies.drain()
    copies.arrived(("back",), back_in, previous)
    cot_arrive[...] = jnp.where(section < lax.axis_size("section") - 1, back_in[...], jnp.zeros_like(back_in[...]))
    for p in "AB":
        cols = pl.ds(base[p], half - rest)
        copies.arrived(("result", p), result_in.at[:, cols], following)
        values = result_in[:, cols]
        fwd_arrive[:, cols] = jnp.where(section > 0, values, jnp.zeros_like(values))
        copies.arrived(("rows", p), fwd_in.at[:, rows_ahead(p)[1]], following)
    for u in range(UNITS - DIRECT, UNITS):
        for i, p in enumerate("AB"):
            here_in = rf.ending(p, u)
            for k in range(RING):
                copies.arrived(("total", p, u, "5", k), here_in.at[k], following)
            lo = i * rest + (u - (UNITS - DIRECT)) * width
            total = here_in[0].astype(f32)
            for k in range(1, RING):
                total += here_in[k].astype(f32)
            values = (fwd_in[:, pl.ds(lo, width)].astype(f32) + total).astype(bf16)
            fwd_arrive[:, rf.cols(p, u)] = jnp.where(section > 0, values, jnp.zeros_like(values))


def tick(fwd, saved, cot, gain, w_in, w_out):
    rows, d = fwd.shape
    ff = w_in.shape[1]
    tokens = rows * RING * RING * PAIR
    half = d // 2
    width = half // UNITS
    slots = 2 * UNITS * 2
    gathered = pltpu.VMEM((RING, RING, PAIR, rows, d), bf16)
    vmem = pl.BlockSpec(memory_space=pltpu.VMEM)
    hbm = pl.BlockSpec(memory_space=pl.ANY)
    n_copies = 3 * 2 * 26 + 2 * UNITS * 2 * 9 + 5
    return pl.pallas_call(
        body,
        out_shape=[
            pltpu.VMEM((rows, d), bf16),
            pltpu.VMEM((rows, d), bf16),
            pltpu.VMEM((d, ff), bf16),
            pltpu.VMEM((ff, d), bf16),
        ],
        in_specs=[hbm, hbm, hbm, vmem, hbm, hbm],
        out_specs=[vmem] * 4,
        scratch_shapes=[
            pltpu.VMEM((d, ff), bf16),
            pltpu.VMEM((ff, d), bf16),
            gathered, gathered, gathered, gathered,
            pltpu.VMEM((sum(CROSS.values()), 2, RING, RING, rows, width), bf16),
            pltpu.VMEM((slots, 2, RING, PAIR, rows, width // 2), bf16),
            pltpu.VMEM((slots, 2, RING, PAIR, rows, width), bf16),
            pltpu.VMEM((slots, RING, rows, width), bf16),
            pltpu.VMEM((slots, 2, rows, width // 2), bf16),
            pltpu.VMEM((slots, 2, rows, width), bf16),
            pltpu.VMEM((tokens, ff), f32),
            pltpu.VMEM((tokens, ff), f32),
            pltpu.VMEM((tokens, ff), bf16),
            pltpu.VMEM((tokens, ff), bf16),
            pltpu.VMEM((tokens, ff), bf16),
            pltpu.VMEM((2, rows, d), f32),
            *[pltpu.VMEM((rows, d), bf16)] * 7,
            pltpu.VMEM((rows, 2 * DIRECT * width), bf16),
            pltpu.VMEM((DIRECT, 2, RING, rows, width), bf16),
            pltpu.SemaphoreType.DMA((n_copies,)),
            pltpu.SemaphoreType.DMA((n_copies,)),
            pltpu.SemaphoreType.DMA((6,)),
        ],
        compiler_params=pltpu.CompilerParams(
            collective_id=0, has_side_effects=True, vmem_limit_bytes=VMEM_MIB * 2**20
        ),
        cost_estimate=pl.CostEstimate(
            flops=14 * tokens * d * ff, bytes_accessed=16 * d * ff, transcendentals=3 * tokens * ff
        ),
    )(fwd, saved, cot, gain, w_in, w_out)


def move(*refs):
    sources, targets, sem = refs[:4], refs[4:8], refs[8]
    copies = [pltpu.make_async_copy(s, t, sem.at[i]) for i, (s, t) in enumerate(zip(sources, targets))]
    for copy in copies:
        copy.start()
    for copy in copies:
        copy.wait()


def placed(*arrays):
    hbm = pl.BlockSpec(memory_space=pl.ANY)
    return pl.pallas_call(
        move,
        out_shape=[pltpu.HBM(a.shape, a.dtype) for a in arrays],
        in_specs=[hbm] * 4,
        out_specs=[hbm] * 4,
        scratch_shapes=[pltpu.SemaphoreType.DMA((4,))],
        compiler_params=pltpu.CompilerParams(vmem_limit_bytes=2 * 2**20),
    )(*arrays)


def per_device(fwd_in, saved, gain, w_in, w_out, cot_in):
    outs = tick(fwd_in[0], saved[0], cot_in[0], gain, w_in[0], w_out[0])
    return tuple(out[None] for out in placed(*outs))


def solution(mesh):
    return jax.shard_map(
        per_device,
        mesh=mesh,
        in_specs=(
            P("section", "fsdp", None),
            P("section", "fsdp", None),
            P("section", None),
            P("section", None, "fsdp"),
            P("section", "fsdp", None),
            P("section", "fsdp", None),
        ),
        out_specs=(
            P("section", "fsdp", None),
            P("section", "fsdp", None),
            P("section", None, "fsdp"),
            P("section", "fsdp", None),
        ),
        check_vma=False,
    )
```
